32 devices in a mesh: frame: 4 (over y, x), row: 2 (over core), chan: 4 (over z).
Axes of the slice: x: 2, y: 2, z: 4, core: 2. Of those that a mesh axis runs over, the one named last changes fastest.
Arguments:
- activations: bfloat16 [320, 12, 2, 128], P('chan', 'frame', 'row'), may hold values from -12 to 12, as said below
- conv_first: bfloat16 [27, 320, 320], P(None, 'chan'), may hold values from -0.0625 to 0.0625
- conv_second: bfloat16 [27, 320, 320], P(None, 'chan'), may hold values from -0.0625 to 0.0625
- cotangent: bfloat16 [320, 12, 2, 128], P('chan', 'frame', 'row'), may hold values from -6 to 6
Outputs:
- result: bfloat16 [320, 12, 2, 128], P('chan', 'frame', 'row')
- input_grad: bfloat16 [320, 12, 2, 128], P('chan', 'frame', 'row')
- first_grad: float32 [27, 320, 320], P(None, 'chan')
- second_grad: float32 [27, 320, 320], P(None, 'chan')
The draws below stay inside these ranges and needn't reach their ends.
Inputs may be any that keep to these rules, and one draw needn't show every extreme that they name: activations of the window.
All inputs are finite; a program needn't handle non-finite values.
Results may differ from the reference program's by a relative error of at most 0.0054.
Values may be sent and summed in bfloat16 or wider, within the bound.
No kernel may reach another device: no remote copies, remote signals or barrier semaphores. Data moves between devices by JAX's collectives and lax.ppermute only.
A program may use at most 128 MiB of HBM per device.

```python
import math
import jax
import jax.numpy as jnp
from jax import lax

C = 320
GROUPS = 32
W = 128
FRAMES = 12
ROWS = 2


def draw_activations(key, part):
    key = jax.random.fold_in(key, 11)
    frame_pos = jnp.arange(FRAMES, dtype=jnp.float32) / max(FRAMES - 1, 1)
    row_pos = jnp.arange(ROWS, dtype=jnp.float32) / max(ROWS - 1, 1)
    factor = jnp.exp(math.log(3.0) * (frame_pos[:, None] - 0.5)) * jnp.exp(math.log(3.0) * (row_pos[None, :] - 0.5))
    base = jnp.clip(jax.random.normal(key, (C, FRAMES, ROWS, W), jnp.float32), -4.0, 4.0)
    return (base * factor[None, :, :, None]).astype(jnp.bfloat16)


def steps_of(rng, extent, cuts, low, top_value):
    def one(position, shards_of):
        steps = jax.random.uniform(jax.random.fold_in(jax.random.fold_in(rng, 6), position), (shards_of,), jnp.float32, low / len(cuts), top_value / len(cuts))
        return jnp.repeat(jnp.exp(steps), extent[position] // shards_of).reshape((-1,) + (1,) * (len(extent) - position - 1))

    gain = one(*cuts[0])
    for cut in cuts[1:]:
        gain = gain * one(*cut)
    return gain


def bell_draw(key, dims, spread, limit, cuts=(), kind=jnp.bfloat16):
    array = spread * jax.random.normal(key, dims, jnp.float32)
    if cuts:
        array = array * steps_of(key, dims, cuts, -0.22, 0.18)
    return jnp.clip(array, -limit, limit).astype(kind)


def setup_inputs(seed: int = 0) -> dict:
    streams_of = jax.random.split(jax.random.key(seed), 5)
    activations = draw_activations(jax.random.fold_in(streams_of[4], 71), 0)
    conv_first = bell_draw(streams_of[1], (27, C, C), (27 * C) ** -0.5, 0.0625, ((1, 4),))
    conv_second = bell_draw(streams_of[2], (27, C, C), (27 * C) ** -0.5, 0.0625, ((1, 4),))
    cotangent = bell_draw(streams_of[3], (C, FRAMES, ROWS, W), 1.0, 6.0, ((0, 4), (1, 4), (2, 2)))
    return {"activations": activations, "conv_first": conv_first, "conv_second": conv_second, "cotangent": cotangent}


EPSILON = 1e-05

def tap_list():
    return [(tap_frame, tap_row, tap_col) for tap_frame in range(3) for tap_row in range(3) for tap_col in range(3)]

def pad_cells(values):
    return jnp.pad(values, ((0, 0), (1, 1), (1, 1), (1, 1)))

def convolve(values, weight):
    channels, frames, height, breadth = values.shape
    padded = pad_cells(values)
    summed = jnp.zeros((weight.shape[2], frames * height * breadth), jnp.float32)
    for tap_index, (tap_frame, tap_row, tap_col) in enumerate(tap_list()):
        window = padded[:, tap_frame:tap_frame + frames, tap_row:tap_row + height, tap_col:tap_col + breadth].reshape(channels, -1)
        summed = summed + jnp.dot(weight[tap_index].T, window, preferred_element_type=jnp.float32)
    return summed

def convolve_back(grads, inputs, weight):
    channels, frames, height, breadth = inputs.shape
    padded_grad = pad_cells(grads)
    padded_input = pad_cells(inputs)
    flat_grad = grads.reshape(grads.shape[0], -1)
    back_sum = jnp.zeros((channels, frames * height * breadth), jnp.float32)
    pieces = []
    for tap_index, (tap_frame, tap_row, tap_col) in enumerate(tap_list()):
        shifted = padded_grad[:, 2 - tap_frame:2 - tap_frame + frames, 2 - tap_row:2 - tap_row + height, 2 - tap_col:2 - tap_col + breadth].reshape(grads.shape[0], -1)
        back_sum = back_sum + jnp.dot(weight[tap_index], shifted, preferred_element_type=jnp.float32)
        window = padded_input[:, tap_frame:tap_frame + frames, tap_row:tap_row + height, tap_col:tap_col + breadth].reshape(channels, -1)
        pieces.append(jnp.dot(window, flat_grad.T, preferred_element_type=jnp.float32))
    return (back_sum, jnp.stack(pieces))

def normalize(summed):
    grouped = summed.reshape(GROUPS, -1)
    average = lax.optimization_barrier(jnp.mean(grouped, axis=1, keepdims=True))
    centered = grouped - average
    variance = lax.optimization_barrier(jnp.mean(centered * centered, axis=1, keepdims=True))
    inv_scale = lax.rsqrt(variance + EPSILON)
    return ((centered * inv_scale).reshape(summed.shape), inv_scale)

def norm_back(grad_norm, normed, inv_scale):
    grouped_grad = grad_norm.reshape(GROUPS, -1)
    grouped_norm = normed.reshape(GROUPS, -1)
    first_mean = lax.optimization_barrier(jnp.mean(grouped_grad, axis=1, keepdims=True))
    second_mean = lax.optimization_barrier(jnp.mean(grouped_grad * grouped_norm, axis=1, keepdims=True))
    return ((grouped_grad - first_mean - grouped_norm * second_mean) * inv_scale).reshape(grad_norm.shape)

def reference(activations, conv_first, conv_second, cotangent):
    layout = activations.shape
    channels = layout[0]
    first_norm, first_scale = normalize(convolve(activations, conv_first))
    first_gate = jax.nn.sigmoid(first_norm)
    hidden = (first_norm * first_gate).astype(jnp.bfloat16).reshape(layout)
    second_norm, second_scale = normalize(convolve(hidden, conv_second))
    second_gate = jax.nn.sigmoid(second_norm)
    result = (activations.astype(jnp.float32).reshape(channels, -1) + second_norm * second_gate).astype(jnp.bfloat16).reshape(layout)
    flat_cot = cotangent.astype(jnp.float32).reshape(channels, -1)
    second_dnorm = flat_cot * second_gate * (1.0 + second_norm * (1.0 - second_gate))
    grad_second = norm_back(second_dnorm, second_norm, second_scale).astype(jnp.bfloat16).reshape(layout)
    hidden_grad, second_grad = convolve_back(grad_second, hidden, conv_second)
    first_dnorm = hidden_grad * first_gate * (1.0 + first_norm * (1.0 - first_gate))
    grad_first = norm_back(first_dnorm, first_norm, first_scale).astype(jnp.bfloat16).reshape(layout)
    conv_back, first_grad = convolve_back(grad_first, activations, conv_first)
    input_grad = (flat_cot + conv_back).astype(jnp.bfloat16).reshape(layout)
    return (result, input_grad, first_grad, second_grad)
```

```python
import functools

import jax
import jax.numpy as jnp
from jax import lax
from jax.experimental import pallas as pl
from jax.experimental.pallas import tpu as pltpu
from jax.sharding import PartitionSpec as P

C = 320
GROUPS = 32


EPSILON = 1e-05
LINK = jnp.float32


def with_halo(cells, sides, width):
    for axis, dim in sides:
        count = lax.axis_size(axis)
        ends = count - 1
        head = lax.slice_in_dim(cells, 0, width, axis=dim)
        tail = lax.slice_in_dim(cells, cells.shape[dim] - width, cells.shape[dim], axis=dim)
        cells = jnp.concatenate(
            [
                lax.ppermute(tail, axis, [(i, (i + 1) % count) for i in range(ends)]),
                cells,
                lax.ppermute(head, axis, [((i + 1) % count, i) for i in range(ends)]),
            ],
            axis=dim,
        )
    return cells


def pad_columns(values):
    return jnp.pad(values, ((0, 0), (0, 0), (0, 0), (1, 1)))


def with_rims(values):
    return with_halo(values, (("frame", 1), ("row", 2)), 1)


def collect(padded, frames, height, breadth, mirrored):
    windows = []
    for tap_frame in range(3):
        for tap_row in range(3):
            for tap_col in range(3):
                if mirrored:
                    anchor = (2 - tap_frame, 2 - tap_row, 2 - tap_col)
                else:
                    anchor = (tap_frame, tap_row, tap_col)
                window = padded[
                    :,
                    anchor[0] : anchor[0] + frames,
                    anchor[1] : anchor[1] + height,
                    anchor[2] : anchor[2] + breadth,
                ]
                windows.append(window.reshape(padded.shape[0], -1))
    return jnp.stack(windows)


def forward_conv(values, weight):
    channels_local, frames, height, breadth = values.shape
    positions = frames * height * breadth
    rimmed = with_rims(values)
    own_patches = collect(pad_columns(rimmed), frames, height, breadth, False)
    flat_own = own_patches.reshape(-1, positions)
    flat_weight = weight.reshape(-1, weight.shape[2])
    summed = lax.psum_scatter(
        lax.dot_general(
            flat_weight, flat_own, (((0,), (0,)), ((), ())), preferred_element_type=jnp.float32
        ),
        "chan",
        scatter_dimension=0,
        tiled=True,
    )
    return (summed, own_patches)


def normalize(summed):
    grouped = summed.reshape(summed.shape[0] // (C // GROUPS), -1)
    members = grouped.shape[1] * lax.axis_size("frame") * lax.axis_size("row")
    totals = lax.psum(jnp.sum(grouped, axis=1), ("frame", "row"))
    average = totals / members
    centered = grouped - average[:, None]
    variance = lax.psum(jnp.sum(centered * centered, axis=1), ("frame", "row")) / members
    inv_scale = lax.rsqrt(variance + EPSILON)
    return ((centered * inv_scale[:, None]).reshape(summed.shape), inv_scale)


def norm_back(grad_norm, normed, inv_scale):
    grouped_grad = grad_norm.reshape(inv_scale.shape[0], -1)
    grouped_norm = normed.reshape(inv_scale.shape[0], -1)
    members = grouped_grad.shape[1] * lax.axis_size("frame") * lax.axis_size("row")
    first_sum, second_sum = lax.psum(
        (jnp.sum(grouped_grad, axis=1), jnp.sum(grouped_grad * grouped_norm, axis=1)),
        ("frame", "row"),
    )
    adjusted = (
        grouped_grad
        - (first_sum / members)[:, None]
        - grouped_norm * (second_sum / members)[:, None]
    )
    return (adjusted * inv_scale[:, None]).reshape(grad_norm.shape)


def back_conv(grads, own_patches, weight):
    channels_local, frames, height, breadth = grads.shape
    positions = frames * height * breadth
    flat_own = own_patches.reshape(-1, positions)
    rimmed = with_rims(grads)
    portion = lax.all_gather(rimmed, "chan", axis=0, tiled=True)
    members = portion.shape[0]
    interior = portion[:, 1:-1, 1:-1, :].reshape(members, -1)
    shifted = collect(pad_columns(portion), frames, height, breadth, True)
    merged_w = jnp.transpose(weight, (1, 0, 2)).reshape(channels_local, -1)
    back_sum = jnp.dot(merged_w, shifted.reshape(-1, positions), preferred_element_type=jnp.float32)
    increment = lax.dot_general(
        flat_own, interior, (((1,), (1,)), ((), ())), preferred_element_type=jnp.float32
    )
    increment = increment.reshape(27, channels_local, members)
    return (back_sum, increment)


def reduce_weights(weight_grad):
    return lax.psum(weight_grad, ("frame", "row"))


def shards_general(activations, conv_first, conv_second, cotangent):
    layout = activations.shape
    channels_local = layout[0]
    first_sum, first_patches = forward_conv(activations, conv_first)
    first_norm, first_scale = normalize(first_sum)
    first_gate = jax.nn.sigmoid(first_norm)
    hidden = (first_norm * first_gate).astype(jnp.bfloat16).reshape(layout)
    second_sum, second_patches = forward_conv(hidden, conv_second)
    second_norm, second_scale = normalize(second_sum)
    second_gate = jax.nn.sigmoid(second_norm)
    result = (
        (activations.astype(jnp.float32).reshape(channels_local, -1) + second_norm * second_gate)
        .astype(jnp.bfloat16)
        .reshape(layout)
    )
    flat_cot = cotangent.astype(jnp.float32).reshape(channels_local, -1)
    second_dnorm = flat_cot * second_gate * (1.0 + second_norm * (1.0 - second_gate))
    grad_second = (
        norm_back(second_dnorm, second_norm, second_scale).astype(jnp.bfloat16).reshape(layout)
    )
    hidden_grad, second_weight = back_conv(grad_second, second_patches, conv_second)
    second_total = reduce_weights(second_weight)
    first_dnorm = hidden_grad * first_gate * (1.0 + first_norm * (1.0 - first_gate))
    grad_first = (
        norm_back(first_dnorm, first_norm, first_scale).astype(jnp.bfloat16).reshape(layout)
    )
    conv_back, first_weight = back_conv(grad_first, first_patches, conv_first)
    first_total = reduce_weights(first_weight)
    input_grad = (flat_cot + conv_back).astype(jnp.bfloat16).reshape(layout)
    return (result, input_grad, first_total, second_total)


BF16 = jnp.bfloat16
F32 = jnp.float32
LANES = 128
HIGH = lax.Precision.HIGHEST
FR = ("frame", "row")


def call(kernel, outs, args, scratch=(), grid=None, specs=None, flops=0, reads=0):
    vmem = pl.BlockSpec(memory_space=pltpu.VMEM)
    in_specs = [pl.BlockSpec(memory_space=pltpu.SMEM)] + [vmem] * (len(args) - 1)
    params = dict(vmem_limit_bytes=60 * 1024 * 1024)
    if grid is not None:
        params["dimension_semantics"] = ("arbitrary",) * len(grid)
    extra = {} if grid is None else {"grid": grid}
    return pl.pallas_call(
        kernel,
        out_shape=outs,
        in_specs=in_specs,
        out_specs=[vmem] * len(outs) if specs is None else specs,
        scratch_shapes=list(scratch),
        compiler_params=pltpu.CompilerParams(**params),
        cost_estimate=pl.CostEstimate(flops=flops, bytes_accessed=reads, transcendentals=0),
        **extra,
    )(*args)


def shift(block, step):
    if step == 1:
        return block
    lane = lax.broadcasted_iota(jnp.int32, block.shape, 1)
    if step == 0:
        moved = pltpu.roll(block, 1, 1)
        return jnp.where(lane == 0, jnp.zeros_like(moved), moved)
    moved = pltpu.roll(block, block.shape[1] - 1, 1)
    return jnp.where(lane == block.shape[1] - 1, jnp.zeros_like(moved), moved)


def fill_patches(patches, block, channels, frames, mirrored, base=0, stride=None):
    stride = channels if stride is None else stride
    for place in range(frames + 2):
        for row in range(2):
            cells = block(place, row)
            pick = 1 - row if mirrored else row
            for tap_col in range(3):
                moved = shift(cells, 2 - tap_col if mirrored else tap_col)
                for tap_frame in range(3):
                    frame = place - 2 + tap_frame if mirrored else place - tap_frame
                    if 0 <= frame < frames:
                        start = ((tap_frame * 2 + pick) * 3 + tap_col) * stride + base
                        if not isinstance(start, int):
                            start = pl.multiple_of(start, 16)
                        patches[pl.ds(start, channels), pl.ds(frame * LANES, LANES)] = moved


def frame_block(place, my_frame, frames, count):
    if place == 0:
        return jnp.maximum(my_frame - 1, 0), frames - 1, my_frame > 0
    if place == frames + 1:
        return jnp.minimum(my_frame + 1, count - 1), 0, my_frame < count - 1
    return my_frame, place - 1, None


def masked(block, keep):
    if keep is None:
        return block
    return jnp.where(keep, block, jnp.zeros_like(block))


def send_slots(total, parts, place, scratch):
    channels = total.shape[0] // 4
    scratch[...] = total
    for slot in range(4):
        owner = jnp.bitwise_xor(place, slot)
        rows = pl.ds(pl.multiple_of(owner * channels, 16), channels)
        parts[slot][...] = scratch[rows, :].astype(parts[slot].dtype)


def group_total(mixer, sums):
    wide = jnp.broadcast_to(sums, (sums.shape[0], LANES))
    return jnp.dot(mixer, wide, precision=HIGH, preferred_element_type=F32)


def first_kernel(frames, where, weight, gathered, p0, p1, p2, p3, patches, total):
    my_frame, place = where[0], where[2]
    count = gathered.shape[0] // 2

    def block(spot, row):
        owner, inner, keep = frame_block(spot, my_frame, frames, count)
        return masked(gathered[owner * 2 + row, 0, :, pl.ds(inner * LANES, LANES)], keep)

    fill_patches(patches, block, gathered.shape[2], frames, False)
    out = jnp.dot(weight[...], patches[...], preferred_element_type=F32)
    send_slots(out, (p0, p1, p2, p3), place, total)


def statistics(sums, mixer, members):
    blocks = sums.shape[0]
    acc = sums[0]
    for k in range(1, blocks):
        acc = acc + sums[k]
    mean = group_total(mixer, jnp.sum(acc, axis=1, keepdims=True))[:, :1] / members
    acc = None
    for k in range(blocks):
        centered = sums[k] - mean
        acc = centered * centered if acc is None else acc + centered * centered
    variance = group_total(mixer, jnp.sum(acc, axis=1, keepdims=True))[:, :1] / members
    return mean, lax.rsqrt(variance + EPSILON)


def second_kernel(
    frames, members, where, weight, mixer, sums, hidden, norm, scale, p0, p1, p2, p3, patches, total
):
    my_frame, my_row, place = where[0], where[1], where[2]
    count = sums.shape[0] // 2
    mean, inv = statistics(sums, mixer[...], members)
    for k in range(sums.shape[0]):
        normed = (sums[k] - mean) * inv
        hidden[k] = (normed * jax.nn.sigmoid(normed)).astype(BF16)
    norm[...] = (sums[my_frame * 2 + my_row] - mean) * inv
    scale[...] = jnp.broadcast_to(inv, scale.shape)

    def block(spot, row):
        owner, inner, keep = frame_block(spot, my_frame, frames, count)
        return masked(hidden[owner * 2 + row, :, pl.ds(inner * LANES, LANES)], keep)

    fill_patches(patches, block, sums.shape[1], frames, False)
    out = jnp.dot(weight[...], patches[...], preferred_element_type=F32)
    send_slots(out, (p0, p1, p2, p3), place, total)


def third_kernel(frames, members, where, mixer, sums, gathered, result, halo, grads, norms, ready):
    my_frame, my_row = where[0], where[1]
    blocks = sums.shape[0]
    count = blocks // 2
    mean, inv = statistics(sums, mixer[...], members)
    first = second = None
    for k in range(blocks):
        normed = (sums[k] - mean) * inv
        gate = jax.nn.sigmoid(normed)
        grad = gathered[k, 1].astype(F32) * gate * (1.0 + normed * (1.0 - gate))
        norms[k] = normed
        grads[k] = grad
        first = grad if first is None else first + grad
        second = grad * normed if second is None else second + grad * normed
    first = group_total(mixer[...], jnp.sum(first, axis=1, keepdims=True))[:, :1] / members
    second = group_total(mixer[...], jnp.sum(second, axis=1, keepdims=True))[:, :1] / members
    for k in range(blocks):
        ready[k] = ((grads[k] - first - norms[k] * second) * inv).astype(BF16)
    own = my_frame * 2 + my_row
    normed = norms[own]
    result[...] = (gathered[own, 0].astype(F32) + normed * jax.nn.sigmoid(normed)).astype(BF16)
    for spot in range(frames + 2):
        owner, inner, keep = frame_block(spot, my_frame, frames, count)
        cells = ready[owner * 2 + my_row, :, pl.ds(inner * LANES, LANES)]
        halo[:, pl.ds(spot * LANES, LANES)] = masked(cells, keep)


def fourth_kernel(frames, where, weight, mine, theirs, norm, grad, sums, patches):
    my_row, place = where[1], where[2]
    channels = mine.shape[1]
    for slot in range(4):
        owner = jnp.bitwise_xor(place, slot)

        def block(spot, row):
            lanes = pl.ds(spot * LANES, LANES)
            return jnp.where(my_row == row, mine[slot, :, lanes], theirs[slot, :, lanes])

        fill_patches(
            patches, block, channels, frames, True, owner * channels, 4 * channels
        )
    out = jnp.dot(weight[...], patches[...], preferred_element_type=F32)
    normed = norm[...]
    gate = jax.nn.sigmoid(normed)
    out = out * gate * (1.0 + normed * (1.0 - gate))
    grad[...] = out
    lane = lax.broadcasted_iota(jnp.int32, sums.shape, 1)
    sums[...] = jnp.where(
        lane == 0,
        jnp.sum(out, axis=1, keepdims=True),
        jnp.where(lane == 1, jnp.sum(out * normed, axis=1, keepdims=True), 0.0),
    )


def fifth_kernel(members, where, mixer, sums, grad, norm, scale, out):
    acc = sums[0]
    for k in range(1, sums.shape[0]):
        acc = acc + sums[k]
    means = jnp.dot(mixer[...], acc, precision=HIGH, preferred_element_type=F32) / members
    out[...] = ((grad[...] - means[:, :1] - norm[...] * means[:, 1:2]) * scale[:, :1]).astype(BF16)


def spread(full, where, frames, pieces):
    my_frame, my_row, place = where[0], where[1], where[2]
    mine, theirs, near, far = pieces
    channels = mine.shape[1]

    def put(row, slot, frame_slot, value):
        owner = jnp.bitwise_xor(place, slot)
        rows = pl.ds(pl.multiple_of(owner * channels, 16), channels)
        width = frames * LANES
        lanes = pl.ds(pl.multiple_of(jnp.bitwise_xor(my_frame, frame_slot) * width, LANES), width)
        full[row, rows, lanes] = value

    for slot in range(4):
        put(my_row, slot, 0, mine[slot])
        put(1 - my_row, slot, 0, theirs[slot])
    for index in range(3):
        for half in range(2):
            for side in range(2):
                put(jnp.bitwise_xor(my_row, side), 2 * my_row + half, index + 1, near[index][side, half])
                put(jnp.bitwise_xor(1 - my_row, side), 2 * (1 - my_row) + half, index + 1, far[index][side, half])


def weight_step(inputs_at, frames, where, pieces, out, padded, full):
    tap_frame = pl.program_id(0)
    total = full.shape[2] // LANES
    count = total // frames

    @pl.when(tap_frame == 0)
    def _():
        spread(full, where, frames, pieces)
        channels = padded.shape[0] // 6
        zeros = jnp.zeros((padded.shape[0], LANES), padded.dtype)
        padded[:, pl.ds(0, LANES)] = zeros
        padded[:, pl.ds((total + 1) * LANES, LANES)] = zeros
        for frame in range(total):
            for row in range(2):
                cells = inputs_at(frame // frames * 2 + row, frame % frames)
                for tap_col in range(3):
                    rows = pl.ds((row * 3 + tap_col) * channels, channels)
                    padded[rows, pl.ds((frame + 1) * LANES, LANES)] = shift(cells, tap_col)

    channels = padded.shape[0] // 6
    window = padded[:, pl.ds(pl.multiple_of(tap_frame * LANES, LANES), total * LANES)]
    top = lax.dot_general(window, full[0], (((1,), (1,)), ((), ())), preferred_element_type=F32)
    low = lax.dot_general(window, full[1], (((1,), (1,)), ((), ())), preferred_element_type=F32)
    for tap_col in range(3):
        upper = slice(tap_col * channels, (tap_col + 1) * channels)
        under = slice((3 + tap_col) * channels, (4 + tap_col) * channels)
        out[tap_col] = low[upper]
        out[3 + tap_col] = top[upper] + low[under]
        out[6 + tap_col] = top[under]


def weight_kernel(frames, where, inputs, mine, theirs, n1, n2, n3, f1, f2, f3, out, padded, full):
    weight_step(
        lambda k, inner: inputs[k, :, pl.ds(inner * LANES, LANES)],
        frames, where, (mine, theirs, (n1, n2, n3), (f1, f2, f3)), out, padded, full,
    )


def last_kernel(
    frames, where, weight, inputs, mine, theirs, n1, n2, n3, f1, f2, f3, out, back, padded, full, patches
):
    weight_step(
        lambda k, inner: inputs[k, 0, :, pl.ds(inner * LANES, LANES)],
        frames, where, (mine, theirs, (n1, n2, n3), (f1, f2, f3)), out, padded, full,
    )

    @pl.when(pl.program_id(0) == 0)
    def _():
        my_frame, my_row = where[0], where[1]
        total = full.shape[2] // LANES

        def block(spot, row):
            frame = my_frame * frames - 1 + spot
            keep = None
            if spot == 0:
                keep = frame >= 0
                frame = jnp.maximum(frame, 0)
            elif spot == frames + 1:
                keep = frame < total
                frame = jnp.minimum(frame, total - 1)
            return masked(full[row, :, pl.ds(pl.multiple_of(frame * LANES, LANES), LANES)], keep)

        fill_patches(patches, block, full.shape[1], frames, True)
        grown = jnp.dot(weight[...], patches[...], preferred_element_type=F32)
        back[...] = (inputs[my_frame * 2 + my_row, 1].astype(F32) + grown).astype(BF16)


def swap(values):
    return lax.ppermute(values, "row", [(0, 1), (1, 0)])


def hop(values, axis, step):
    return lax.ppermute(values, axis, [(i, i ^ step) for i in range(4)])


def over_channels(parts):
    return parts[0] + sum(hop(parts[k], "chan", k).astype(F32) for k in range(1, 4))


def exchange(mine, theirs, my_row):
    both = jnp.stack([mine, theirs])
    half = lax.dynamic_slice_in_dim(both, 2 * my_row, 2, axis=1)
    near = [hop(half, "frame", k) for k in range(1, 4)]
    return near, [swap(values) for values in near]


def shards_paired(activations, conv_first, conv_second, cotangent):
    layout = activations.shape
    channels, frames = layout[0], layout[1]
    cells = frames * LANES
    count = lax.axis_size("frame")
    wide = 4 * channels
    members = (C // GROUPS) * cells * count * 2
    my_frame, my_row, place = (lax.axis_index(a) for a in ("frame", "row", "chan"))
    where = jnp.stack([my_frame, my_row, place]).astype(jnp.int32)
    group = jnp.arange(channels) // (C // GROUPS)
    mixer = (group[:, None] == group[None, :]).astype(F32)
    conv_cost = dict(flops=2 * channels * wide * 18 * cells, reads=18 * channels * wide * 2)

    def ahead(weight):
        taps = lax.dynamic_slice_in_dim(weight.reshape(3, 3, 3, channels, wide), 1 - my_row, 2, axis=1)
        return taps.reshape(18 * channels, wide).T

    def behind(weight):
        taps = lax.dynamic_slice_in_dim(weight.reshape(3, 3, 3, channels, wide), my_row, 2, axis=1)
        return taps.transpose(3, 0, 1, 2, 4).reshape(channels, 18 * wide)

    sums_shape = jax.ShapeDtypeStruct((channels, cells), F32)
    cells_shape = jax.ShapeDtypeStruct((channels, cells), BF16)
    parts_shape = [sums_shape] + [jax.ShapeDtypeStruct((channels, cells), LINK)] * 3
    patches = pltpu.VMEM((18 * channels, cells), BF16)
    wide_patches = pltpu.VMEM((18 * wide, cells), BF16)
    total = pltpu.VMEM((wide, cells), F32)

    pair = jnp.stack([activations.reshape(channels, cells), cotangent.reshape(channels, cells)])
    gathered = lax.all_gather(pair, FR, axis=0)
    parts = call(
        functools.partial(first_kernel, frames), parts_shape,
        (where, ahead(conv_first), gathered), (patches, total), **conv_cost,
    )
    first_sums = lax.all_gather(over_channels(parts), FR, axis=0)
    hidden, norm, scale, *parts = call(
        functools.partial(second_kernel, frames, members),
        [
            jax.ShapeDtypeStruct((2 * count, channels, cells), BF16),
            sums_shape,
            jax.ShapeDtypeStruct((channels, LANES), F32),
            *parts_shape,
        ],
        (where, ahead(conv_second), mixer, first_sums), (patches, total), **conv_cost,
    )
    second_sums = lax.all_gather(over_channels(parts), FR, axis=0)
    blocks = (2 * count, channels, cells)
    result, halo = call(
        functools.partial(third_kernel, frames, members),
        [cells_shape, jax.ShapeDtypeStruct((channels, cells + 2 * LANES), BF16)],
        (where, mixer, second_sums, gathered),
        (pltpu.VMEM(blocks, F32), pltpu.VMEM(blocks, F32), pltpu.VMEM(blocks, BF16)),
    )
    mine = jnp.stack([halo] + [hop(halo, "chan", k) for k in range(1, 4)])
    theirs = swap(mine)
    grad, sums = call(
        functools.partial(fourth_kernel, frames),
        [sums_shape, jax.ShapeDtypeStruct((channels, LANES), F32)],
        (where, behind(conv_second), mine, theirs, norm), (wide_patches,), **conv_cost,
    )
    own_mine = mine[:, :, LANES:-LANES]
    own_theirs = theirs[:, :, LANES:-LANES]
    near, far = exchange(own_mine, own_theirs, my_row)

    sums = lax.all_gather(sums, FR, axis=0)
    (grad_first,) = call(
        functools.partial(fifth_kernel, members), [cells_shape], (where, mixer, sums, grad, norm, scale)
    )
    padded = pltpu.VMEM((6 * channels, (frames * count + 2) * LANES), BF16)
    full = pltpu.VMEM((2, wide, cells * count), BF16)
    grad_shape = jax.ShapeDtypeStruct((27, channels, wide), F32)
    grad_spec = pl.BlockSpec((9, channels, wide), lambda a: (a, 0, 0))
    grad_cost = dict(flops=2 * 18 * channels * wide * cells * count * 2, reads=8000000)
    (second_grad,) = call(
        functools.partial(weight_kernel, frames), [grad_shape],
        (where, hidden, own_mine, own_theirs, *near, *far), (padded, full),
        grid=(3,), specs=[grad_spec], **grad_cost,
    )
    mine = jnp.stack([grad_first] + [hop(grad_first, "chan", k) for k in range(1, 4)])
    theirs = swap(mine)
    near, far = exchange(mine, theirs, my_row)
    first_grad, input_grad = call(
        functools.partial(last_kernel, frames), [grad_shape, cells_shape],
        (where, behind(conv_first), gathered, mine, theirs, *near, *far), (padded, full, wide_patches),
        grid=(3,), specs=[grad_spec, pl.BlockSpec((channels, cells), lambda a: (0, 0))], **grad_cost,
    )
    return (result.reshape(layout), input_grad.reshape(layout), first_grad, second_grad)


def paired(mesh):
    return mesh.shape["frame"] == 4 and mesh.shape["row"] == 2 and mesh.shape["chan"] == 4


def solution(mesh):
    return jax.shard_map(
        shards_paired if paired(mesh) else shards_general,
        mesh=mesh,
        in_specs=(
            P("chan", "frame", "row", None),
            P(None, "chan", None),
            P(None, "chan", None),
            P("chan", "frame", "row", None),
        ),
        out_specs=(
            P("chan", "frame", "row", None),
            P("chan", "frame", "row", None),
            P(None, "chan", None),
            P(None, "chan", None),
        ),
        check_vma=False,
    )
```

```python
import functools

import jax
import jax.numpy as jnp
import numpy as np
from jax import lax
from jax.experimental import pallas as pl
from jax.experimental.pallas import tpu as pltpu
from jax.sharding import PartitionSpec as P

C = 320
GROUPS = 32


EPSILON = 1e-05
LINK = jnp.bfloat16


def with_halo(cells, sides, width):
    for axis, dim in sides:
        count = lax.axis_size(axis)
        ends = count - 1
        head = lax.slice_in_dim(cells, 0, width, axis=dim)
        tail = lax.slice_in_dim(cells, cells.shape[dim] - width, cells.shape[dim], axis=dim)
        cells = jnp.concatenate(
            [
                lax.ppermute(tail, axis, [(i, (i + 1) % count) for i in range(ends)]),
                cells,
                lax.ppermute(head, axis, [((i + 1) % count, i) for i in range(ends)]),
            ],
            axis=dim,
        )
    return cells


def pad_columns(values):
    return jnp.pad(values, ((0, 0), (0, 0), (0, 0), (1, 1)))


def with_rims(values):
    return with_halo(values, (("frame", 1), ("row", 2)), 1)


def collect(padded, frames, height, breadth, mirrored):
    windows = []
    for tap_frame in range(3):
        for tap_row in range(3):
            for tap_col in range(3):
                if mirrored:
                    anchor = (2 - tap_frame, 2 - tap_row, 2 - tap_col)
                else:
                    anchor = (tap_frame, tap_row, tap_col)
                window = padded[
                    :,
                    anchor[0] : anchor[0] + frames,
                    anchor[1] : anchor[1] + height,
                    anchor[2] : anchor[2] + breadth,
                ]
                windows.append(window.reshape(padded.shape[0], -1))
    return jnp.stack(windows)


def forward_conv(values, weight):
    channels_local, frames, height, breadth = values.shape
    positions = frames * height * breadth
    rimmed = with_rims(values)
    own_patches = collect(pad_columns(rimmed), frames, height, breadth, False)
    flat_own = own_patches.reshape(-1, positions)
    flat_weight = weight.reshape(-1, weight.shape[2])
    summed = lax.psum_scatter(
        lax.dot_general(
            flat_weight, flat_own, (((0,), (0,)), ((), ())), preferred_element_type=jnp.float32
        ),
        "chan",
        scatter_dimension=0,
        tiled=True,
    )
    return (summed, own_patches)


def normalize(summed):
    grouped = summed.reshape(summed.shape[0] // (C // GROUPS), -1)
    members = grouped.shape[1] * lax.axis_size("frame") * lax.axis_size("row")
    totals = lax.psum(jnp.sum(grouped, axis=1), ("frame", "row"))
    average = totals / members
    centered = grouped - average[:, None]
    variance = lax.psum(jnp.sum(centered * centered, axis=1), ("frame", "row")) / members
    inv_scale = lax.rsqrt(variance + EPSILON)
    return ((centered * inv_scale[:, None]).reshape(summed.shape), inv_scale)


def norm_back(grad_norm, normed, inv_scale):
    grouped_grad = grad_norm.reshape(inv_scale.shape[0], -1)
    grouped_norm = normed.reshape(inv_scale.shape[0], -1)
    members = grouped_grad.shape[1] * lax.axis_size("frame") * lax.axis_size("row")
    first_sum, second_sum = lax.psum(
        (jnp.sum(grouped_grad, axis=1), jnp.sum(grouped_grad * grouped_norm, axis=1)),
        ("frame", "row"),
    )
    adjusted = (
        grouped_grad
        - (first_sum / members)[:, None]
        - grouped_norm * (second_sum / members)[:, None]
    )
    return (adjusted * inv_scale[:, None]).reshape(grad_norm.shape)


def back_conv(grads, own_patches, weight):
    channels_local, frames, height, breadth = grads.shape
    positions = frames * height * breadth
    flat_own = own_patches.reshape(-1, positions)
    rimmed = with_rims(grads)
    portion = lax.all_gather(rimmed, "chan", axis=0, tiled=True)
    members = portion.shape[0]
    interior = portion[:, 1:-1, 1:-1, :].reshape(members, -1)
    shifted = collect(pad_columns(portion), frames, height, breadth, True)
    merged_w = jnp.transpose(weight, (1, 0, 2)).reshape(channels_local, -1)
    back_sum = jnp.dot(merged_w, shifted.reshape(-1, positions), preferred_element_type=jnp.float32)
    increment = lax.dot_general(
        flat_own, interior, (((1,), (1,)), ((), ())), preferred_element_type=jnp.float32
    )
    increment = increment.reshape(27, channels_local, members)
    return (back_sum, increment)


def reduce_weights(weight_grad):
    return lax.psum(weight_grad, ("frame", "row"))


def shards_general(activations, conv_first, conv_second, cotangent):
    layout = activations.shape
    channels_local = layout[0]
    first_sum, first_patches = forward_conv(activations, conv_first)
    first_norm, first_scale = normalize(first_sum)
    first_gate = jax.nn.sigmoid(first_norm)
    hidden = (first_norm * first_gate).astype(jnp.bfloat16).reshape(layout)
    second_sum, second_patches = forward_conv(hidden, conv_second)
    second_norm, second_scale = normalize(second_sum)
    second_gate = jax.nn.sigmoid(second_norm)
    result = (
        (activations.astype(jnp.float32).reshape(channels_local, -1) + second_norm * second_gate)
        .astype(jnp.bfloat16)
        .reshape(layout)
    )
    flat_cot = cotangent.astype(jnp.float32).reshape(channels_local, -1)
    second_dnorm = flat_cot * second_gate * (1.0 + second_norm * (1.0 - second_gate))
    grad_second = (
        norm_back(second_dnorm, second_norm, second_scale).astype(jnp.bfloat16).reshape(layout)
    )
    hidden_grad, second_weight = back_conv(grad_second, second_patches, conv_second)
    second_total = reduce_weights(second_weight)
    first_dnorm = hidden_grad * first_gate * (1.0 + first_norm * (1.0 - first_gate))
    grad_first = (
        norm_back(first_dnorm, first_norm, first_scale).astype(jnp.bfloat16).reshape(layout)
    )
    conv_back, first_weight = back_conv(grad_first, first_patches, conv_first)
    first_total = reduce_weights(first_weight)
    input_grad = (flat_cot + conv_back).astype(jnp.bfloat16).reshape(layout)
    return (result, input_grad, first_total, second_total)


BF16 = jnp.bfloat16
F32 = jnp.float32
LANES = 128
HIGH = lax.Precision.HIGHEST
SIDES = [(slot, side) for slot in range(4) for side in range(2)]


def call(kernel, outs, args, scratch=(), grid=None, specs=None, flops=0, reads=0, grant=16, after=()):
    vmem = pl.BlockSpec(memory_space=pltpu.VMEM)
    in_specs = [pl.BlockSpec(memory_space=pltpu.SMEM)] + [vmem] * (len(args) - 1)
    if after:
        inner, taken = kernel, len(args)
        kernel = lambda *refs: inner(*refs[:taken], *refs[taken + len(after) :])
        in_specs += [pl.BlockSpec(memory_space=pl.ANY)] * len(after)
        args = (*args, *after)
    params = dict(vmem_limit_bytes=grant * 1024 * 1024)
    if grid is not None:
        params["dimension_semantics"] = ("arbitrary",) * len(grid)
    extra = {} if grid is None else {"grid": grid}
    return pl.pallas_call(
        kernel,
        out_shape=outs,
        in_specs=in_specs,
        out_specs=[vmem] * len(outs) if specs is None else specs,
        scratch_shapes=list(scratch),
        compiler_params=pltpu.CompilerParams(**params),
        cost_estimate=pl.CostEstimate(flops=flops, bytes_accessed=reads, transcendentals=0),
        **extra,
    )(*args)


def shift(block, step):
    if step == 1:
        return block
    lane = lax.broadcasted_iota(jnp.int32, block.shape, 1)
    if step == 0:
        moved = pltpu.roll(block, 1, 1)
        return jnp.where(lane == 0, jnp.zeros_like(moved), moved)
    moved = pltpu.roll(block, block.shape[1] - 1, 1)
    return jnp.where(lane == block.shape[1] - 1, jnp.zeros_like(moved), moved)


def fill_shifted(shifted, block, channels, frames, mirrored, base=0, stride=None):
    stride = channels if stride is None else stride
    for place in range(frames + 2):
        for side in range(2):
            cells = block(place, side)
            for tap_col in range(3):
                start = (side * 3 + tap_col) * stride + base
                if not isinstance(start, int):
                    start = pl.multiple_of(start, 16)
                lanes = pl.ds(place * LANES, LANES)
                shifted[pl.ds(start, channels), lanes] = shift(cells, 2 - tap_col if mirrored else tap_col)


def neighbour_block(pieces, place, side, frames, where):
    my_frame = where[0]
    if place == 0:
        cells = jnp.where(my_frame == 2, pieces(3, side, frames - 1), pieces(1, side, frames - 1))
        return jnp.where(my_frame > 0, cells, jnp.zeros_like(cells))
    if place == frames + 1:
        cells = jnp.where(my_frame == 1, pieces(3, side, 0), pieces(1, side, 0))
        return jnp.where(my_frame < 3, cells, jnp.zeros_like(cells))
    return pieces(0, side, place - 1)


def pick(refs):
    return lambda slot, side, frame: refs[2 * slot + side][frame]


def other_tap(where, mirrored):
    return 2 * where[1] if mirrored else 2 - 2 * where[1]


def prepare_kernel(where, first, second, behind_first, behind_second):
    for weight, behind in ((first, behind_first), (second, behind_second)):
        for tap_frame in range(3):
            for side in range(2):
                row = other_tap(where, True) if side else 1
                taps = [weight[9 * tap_frame + 3 * row + tap_col] for tap_col in range(3)]
                behind[tap_frame * 2 + side] = jnp.concatenate(taps, axis=1)


def forward_product(where, weight, shifted, parts, scratch, frames):
    channels, wide = weight.shape[1:]
    out = None
    for tap_frame in range(3):
        for side in range(2):
            row = other_tap(where, False) if side else 1
            taps = weight[pl.ds(9 * tap_frame + 3 * row, 3)].reshape(3 * channels, wide)
            window = shifted[
                pl.ds(side * 3 * channels, 3 * channels), pl.ds(tap_frame * LANES, frames * LANES)
            ]
            term = lax.dot_general(
                taps, window, (((0,), (0,)), ((), ())), preferred_element_type=F32
            )
            out = term if out is None else out + term
    scratch[...] = out
    for slot in range(4):
        owner = jnp.bitwise_xor(where[2], slot)
        rows = pl.ds(pl.multiple_of(owner * channels, 16), channels)
        for frame in range(frames):
            cells = scratch[rows, pl.ds(frame * LANES, LANES)]
            parts[slot][frame] = cells.astype(parts[slot].dtype)


def group_total(mixer, sums):
    wide = jnp.broadcast_to(sums, (sums.shape[0], LANES))
    return jnp.dot(mixer, wide, precision=HIGH, preferred_element_type=F32)


def first_kernel(frames, where, weight, *rest):
    pieces, parts, (shifted, total) = rest[:8], rest[8:12], rest[12:]
    block = lambda place, side: neighbour_block(pick(pieces), place, side, frames, where)
    fill_shifted(shifted, block, weight.shape[1], frames, False)
    forward_product(where, weight, shifted, parts, total, frames)


def statistics(sums, mixer, members):
    acc = None
    for block in sums:
        for frame in range(block.shape[0]):
            acc = block[frame] if acc is None else acc + block[frame]
    mean = group_total(mixer, jnp.sum(acc, axis=1, keepdims=True))[:, :1] / members
    acc = None
    for block in sums:
        for frame in range(block.shape[0]):
            centered = block[frame] - mean
            acc = centered * centered if acc is None else acc + centered * centered
    variance = group_total(mixer, jnp.sum(acc, axis=1, keepdims=True))[:, :1] / members
    return mean, lax.rsqrt(variance + EPSILON)


def second_kernel(frames, members, where, weight, mixer, *rest):
    sums, (hidden, norm, scale), parts, (shifted, total) = rest[:8], rest[8:11], rest[11:15], rest[15:]
    mean, inv = statistics(sums, mixer[...], members)
    for slot, side in SIDES:
        for frame in range(frames):
            normed = (sums[2 * slot + side][frame] - mean) * inv
            hidden[slot, side, frame] = (normed * jax.nn.sigmoid(normed)).astype(BF16)
            if slot == 0 and side == 0:
                norm[frame] = normed
    lane = lax.broadcasted_iota(jnp.int32, scale.shape, 1)
    scale[...] = jnp.where(lane == 0, mean, inv)
    at = lambda slot, side, frame: hidden[slot, side, frame]
    block = lambda place, side: neighbour_block(at, place, side, frames, where)
    fill_shifted(shifted, block, mixer.shape[0], frames, False)
    forward_product(where, weight, shifted, parts, total, frames)


def third_kernel(frames, members, where, mixer, *rest):
    sums, given, own, (result, halo, every, grads, norms) = rest[:8], rest[8:16], rest[16], rest[17:]
    mean, inv = statistics(sums, mixer[...], members)
    first = second = None
    for slot, side in SIDES:
        for frame in range(frames):
            normed = (sums[2 * slot + side][frame] - mean) * inv
            gate = jax.nn.sigmoid(normed)
            grad = given[2 * slot + side][frame].astype(F32) * gate * (1.0 + normed * (1.0 - gate))
            first = grad if first is None else first + grad
            second = grad * normed if second is None else second + grad * normed
            norms[slot, side, frame] = normed
            grads[slot, side, frame] = grad
            if slot == 0 and side == 0:
                result[frame] = (own[frame].astype(F32) + normed * gate).astype(BF16)
    first = group_total(mixer[...], jnp.sum(first, axis=1, keepdims=True))[:, :1] / members
    second = group_total(mixer[...], jnp.sum(second, axis=1, keepdims=True))[:, :1] / members
    for slot, side in SIDES:
        for frame in range(frames):
            cells = grads[slot, side, frame] - first - norms[slot, side, frame] * second
            every[slot, side, frame] = (cells * inv).astype(BF16)
    ready = lambda slot, side, frame: every[slot, side, frame]
    for place in range(frames + 2):
        halo[place] = neighbour_block(ready, place, 0, frames, where)


def fourth_kernel(frames, where, weight, norm, *rest):
    halos, (grad, shifted) = rest[:8], rest[8:]
    channels = norm.shape[1]
    for part in range(4):
        owner = jnp.bitwise_xor(where[2], part)
        block = lambda place, side: halos[2 * part + side][place]
        fill_shifted(shifted, block, channels, frames, True, owner * channels, 4 * channels)
    out = back_product(weight, shifted, frames)
    for frame in range(frames):
        normed = norm[frame]
        gate = jax.nn.sigmoid(normed)
        cells = out[:, frame * LANES : (frame + 1) * LANES]
        grad[frame] = cells * gate * (1.0 + normed * (1.0 - gate))


def back_product(weight, shifted, frames):
    depth = weight.shape[2]
    out = None
    for tap_frame in range(3):
        for side in range(2):
            window = shifted[
                pl.ds(side * depth, depth), pl.ds((2 - tap_frame) * LANES, frames * LANES)
            ]
            term = jnp.dot(weight[tap_frame * 2 + side], window, preferred_element_type=F32)
            out = term if out is None else out + term
    return out


def fifth_kernel(frames, members, where, mixer, scale, *rest):
    sums, grads, (out, every) = rest[:8], rest[8:16], rest[16:]
    mean, inv = scale[:, :1], scale[:, 1:2]
    norm = lambda slot, side, frame: (sums[2 * slot + side][frame] - mean) * inv
    first = second = None
    for slot, side in SIDES:
        for frame in range(frames):
            cells = grads[2 * slot + side][frame]
            first = cells if first is None else first + cells
            term = cells * norm(slot, side, frame)
            second = term if second is None else second + term
    first = group_total(mixer[...], jnp.sum(first, axis=1, keepdims=True))[:, :1] / members
    second = group_total(mixer[...], jnp.sum(second, axis=1, keepdims=True))[:, :1] / members
    for slot, side in SIDES:
        for frame in range(frames):
            cells = grads[2 * slot + side][frame] - first - norm(slot, side, frame) * second
            cells = (cells * inv).astype(BF16)
            every[slot, side, frame] = cells
            if slot == 0 and side == 0:
                out[frame] = cells


def pad_kernel(frames, where, *rest):
    pieces, padded = rest[:8], rest[8]
    fill_padded(padded, pick(pieces), frames, where, pieces[0].shape[1])


def lanes_of(where, slot, frames, frame):
    start = jnp.bitwise_xor(where[0], slot) * frames + frame
    return pl.ds(pl.multiple_of(start * LANES, LANES), LANES)


def fill_padded(padded, inputs, frames, where, channels):
    zeros = jnp.zeros((padded.shape[0], LANES), padded.dtype)
    padded[:, pl.ds(0, LANES)] = zeros
    padded[:, pl.ds(padded.shape[1] - LANES, LANES)] = zeros
    for slot, side in SIDES:
        for frame in range(frames):
            cells = inputs(slot, side, frame)
            for tap_col in range(3):
                rows = pl.ds((side * 3 + tap_col) * channels, channels)
                padded[rows, lanes_of(where, slot, frames, frame + 1)] = shift(cells, tap_col)


def weight_step(grads, frames, where, channels, out, padded, full, prologue):
    tap_frame = pl.program_id(0)
    under_rows = -(-4 * channels // LANES) * LANES

    @pl.when(tap_frame == 0)
    def _():
        prologue()
        gap = under_rows - 4 * channels
        full[pl.ds(4 * channels, gap), :] = jnp.zeros((gap, full.shape[1]), full.dtype)
        for slot, side in SIDES:
            for frame in range(frames):
                for part in range(4):
                    owner = jnp.bitwise_xor(where[2], part)
                    rows = pl.ds(pl.multiple_of(side * under_rows + owner * channels, 16), channels)
                    full[rows, lanes_of(where, slot, frames, frame)] = grads(slot, side, part, frame)

    window = padded[:, pl.ds(pl.multiple_of(tap_frame * LANES, LANES), full.shape[1])]
    both = lax.dot_general(window, full[...], (((1,), (1,)), ((), ())), preferred_element_type=F32)
    mine, theirs = both[:, : 4 * channels], both[:, under_rows:]
    for tap_col in range(3):
        upper = slice(tap_col * channels, (tap_col + 1) * channels)
        under = slice((3 + tap_col) * channels, (4 + tap_col) * channels)
        out[3 + tap_col] = mine[upper] + theirs[under]
        out[3 * other_tap(where, False) + tap_col] = mine[under]
        out[3 * other_tap(where, True) + tap_col] = theirs[upper]


def weight_kernel(frames, where, hidden, every, *rest):
    own, far, (out, padded, full) = rest[:6], rest[6:12], rest[12:]
    channels = hidden.shape[3]

    def grads(slot, side, part, frame):
        if part == 0:
            return every[slot, side, frame]
        if slot == 0:
            return own[2 * (part - 1) + side][frame + 1]
        return far[2 * (slot - 1) + side][part - 1, frame]

    inputs = lambda slot, side, frame: hidden[slot, side, frame]
    prologue = lambda: fill_padded(padded, inputs, frames, where, channels)
    weight_step(grads, frames, where, channels, out, padded, full, prologue)


def last_kernel(frames, where, weight, cotangent, padded, every, *rest):
    far, (out, back, full, shifted) = rest[:8], rest[8:]
    channels = weight.shape[1]

    def grads(slot, side, part, frame):
        if part == 0:
            return every[slot, side, frame]
        return far[2 * slot + side][part - 1, frame]

    def prologue():
        for part in range(4):
            pieces = lambda slot, side, frame: grads(slot, side, part, frame)
            block = lambda place, side: neighbour_block(pieces, place, side, frames, where)
            owner = jnp.bitwise_xor(where[2], part)
            fill_shifted(shifted, block, channels, frames, True, owner * channels, 4 * channels)
        grown = back_product(weight, shifted, frames)
        for frame in range(frames):
            cells = cotangent[frame].astype(F32) + grown[:, frame * LANES : (frame + 1) * LANES]
            back[frame] = cells.astype(BF16)

    weight_step(grads, frames, where, channels, out, padded, full, prologue)


def swap(values):
    return lax.ppermute(values, "row", [(0, 1), (1, 0)])


def hop(values, axis, step):
    return lax.ppermute(values, axis, [(i, i ^ step) for i in range(4)])


def over_channels(parts):
    return parts[0] + sum(hop(parts[k], "chan", k).astype(F32) for k in range(1, 4))


def hops(values):
    return [hop(values, "frame", k) for k in range(1, 4)]


def with_sides(pieces):
    return [values for piece in pieces for values in (piece, swap(piece))]


def around(values):
    return with_sides([values] + hops(values))


def shards_paired(activations, conv_first, conv_second, cotangent):
    channels, frames = activations.shape[:2]
    cells = frames * LANES
    count = lax.axis_size("frame")
    wide = 4 * channels
    members = (C // GROUPS) * cells * count * 2
    my_frame, my_row, place = (lax.axis_index(a) for a in ("frame", "row", "chan"))
    where = jnp.stack([my_frame, my_row, place]).astype(jnp.int32)
    group = np.arange(channels) // (C // GROUPS)
    mixer = jnp.asarray((group[:, None] == group[None, :]).astype(np.float32))
    conv_cost = dict(flops=2 * channels * wide * 18 * cells, reads=18 * channels * wide * 2)

    block = (frames, channels, LANES)
    sums_shape = jax.ShapeDtypeStruct(block, F32)
    cells_shape = jax.ShapeDtypeStruct(block, BF16)
    parts_shape = [sums_shape] + [jax.ShapeDtypeStruct(block, LINK)] * 3
    span = (frames + 2) * LANES
    shifted = pltpu.VMEM((6 * channels, span), BF16)
    wide_shifted = pltpu.VMEM((6 * wide, span), BF16)
    total = pltpu.VMEM((wide, cells), F32)

    by_frame = lambda values: values.transpose(1, 2, 0, 3).reshape(block)
    restore = lambda values: values.reshape(frames, 1, channels, LANES).transpose(2, 0, 1, 3)
    inputs, given = by_frame(activations), by_frame(cotangent)
    behind_shape = jax.ShapeDtypeStruct((6, channels, 3 * wide), BF16)
    prepared = call(
        prepare_kernel, [behind_shape, behind_shape], (where, conv_first, conv_second), reads=6000000
    )
    near, (behind_first, behind_second) = lax.optimization_barrier((hops(inputs), prepared))
    every_input = with_sides([inputs] + near)
    parts = call(
        functools.partial(first_kernel, frames), parts_shape,
        (where, conv_first, *every_input), (shifted, total), **conv_cost,
    )
    given, parts = lax.optimization_barrier((given, parts))
    near, sums = lax.optimization_barrier((hops(given), over_channels(parts)))
    every_given = with_sides([given] + near)
    first_sums = around(sums)
    hidden, norm, scale, *parts = call(
        functools.partial(second_kernel, frames, members),
        [
            jax.ShapeDtypeStruct((count, 2, *block), BF16),
            sums_shape,
            jax.ShapeDtypeStruct((channels, LANES), F32),
            *parts_shape,
        ],
        (where, conv_second, mixer, *first_sums), (shifted, total), **conv_cost,
    )
    second_sums = around(over_channels(parts))
    every_shape = jax.ShapeDtypeStruct((count, 2, *block), BF16)
    result, halo, every_second = call(
        functools.partial(third_kernel, frames, members),
        [cells_shape, jax.ShapeDtypeStruct((frames + 2, channels, LANES), BF16), every_shape],
        (where, mixer, *second_sums, *every_given, inputs),
        (pltpu.VMEM((4, 2, *block), F32), pltpu.VMEM((4, 2, *block), F32)), grant=24,
    )
    halos = [halo] + [hop(halo, "chan", k) for k in range(1, 4)]
    sides = with_sides(halos)
    (grad,) = call(
        functools.partial(fourth_kernel, frames), [sums_shape],
        (where, behind_second, norm, *sides), (wide_shifted,), **conv_cost,
    )
    grad_first, every_first = call(
        functools.partial(fifth_kernel, frames, members), [cells_shape, every_shape],
        (where, mixer, scale, *first_sums, *around(grad)),
    )
    rest = jnp.stack([values[1:-1] for values in halos[1:]])
    rest, grad_first = lax.optimization_barrier((rest, grad_first))
    padded_shape = jax.ShapeDtypeStruct((6 * channels, (frames * count + 2) * LANES), BF16)
    padded = pltpu.VMEM(padded_shape.shape, BF16)
    full = pltpu.VMEM((-(-wide // LANES) * LANES + wide, cells * count), BF16)
    grad_shape = jax.ShapeDtypeStruct((27, channels, wide), F32)
    grad_spec = pl.BlockSpec((9, channels, wide), lambda a: (a, 0, 0))
    grad_cost = dict(flops=2 * 18 * channels * wide * cells * count * 2, reads=8000000)
    (second_grad,) = call(
        functools.partial(weight_kernel, frames), [grad_shape],
        (where, hidden, every_second, *sides[2:], *with_sides(hops(rest))), (padded, full),
        grid=(3,), specs=[grad_spec], grant=32, **grad_cost,
    )
    (padded_inputs,) = call(
        functools.partial(pad_kernel, frames), [padded_shape], (where, *every_input), reads=2000000
    )
    rest = jnp.stack([hop(grad_first, "chan", k) for k in range(1, 4)])
    near, (second_grad, padded_inputs) = lax.optimization_barrier(
        (hops(rest), (second_grad, padded_inputs))
    )
    first_grad, input_grad = call(
        functools.partial(last_kernel, frames), [grad_shape, cells_shape],
        (where, behind_first, given, padded_inputs, every_first, *with_sides([rest] + near)),
        (full, wide_shifted), grid=(3,),
        specs=[grad_spec, pl.BlockSpec(block, lambda a: (0, 0, 0))], grant=32, **grad_cost,
    )
    return (restore(result), restore(input_grad), first_grad, second_grad)


def paired(mesh):
    return mesh.shape["frame"] == 4 and mesh.shape["row"] == 2 and mesh.shape["chan"] == 4


def solution(mesh):
    return jax.shard_map(
        shards_paired if paired(mesh) else shards_general,
        mesh=mesh,
        in_specs=(
            P("chan", "frame", "row", None),
            P(None, "chan", None),
            P(None, "chan", None),
            P("chan", "frame", "row", None),
        ),
        out_specs=(
            P("chan", "frame", "row", None),
            P("chan", "frame", "row", None),
            P(None, "chan", None),
            P(None, "chan", None),
        ),
        check_vma=False,
    )
```

```python
import functools

import jax
import jax.numpy as jnp
import numpy as np
from jax import lax
from jax.experimental import pallas as pl
from jax.experimental.pallas import tpu as pltpu
from jax.sharding import PartitionSpec as P

C = 320
GROUPS = 32


EPSILON = 1e-05
LINK = jnp.bfloat16


def with_halo(cells, sides, width):
    for axis, dim in sides:
        count = lax.axis_size(axis)
        ends = count - 1
        head = lax.slice_in_dim(cells, 0, width, axis=dim)
        tail = lax.slice_in_dim(cells, cells.shape[dim] - width, cells.shape[dim], axis=dim)
        cells = jnp.concatenate(
            [
                lax.ppermute(tail, axis, [(i, (i + 1) % count) for i in range(ends)]),
                cells,
                lax.ppermute(head, axis, [((i + 1) % count, i) for i in range(ends)]),
            ],
            axis=dim,
        )
    return cells


def pad_columns(values):
    return jnp.pad(values, ((0, 0), (0, 0), (0, 0), (1, 1)))


def with_rims(values):
    return with_halo(values, (("frame", 1), ("row", 2)), 1)


def collect(padded, frames, height, breadth, mirrored):
    windows = []
    for tap_frame in range(3):
        for tap_row in range(3):
            for tap_col in range(3):
                if mirrored:
                    anchor = (2 - tap_frame, 2 - tap_row, 2 - tap_col)
                else:
                    anchor = (tap_frame, tap_row, tap_col)
                window = padded[
                    :,
                    anchor[0] : anchor[0] + frames,
                    anchor[1] : anchor[1] + height,
                    anchor[2] : anchor[2] + breadth,
                ]
                windows.append(window.reshape(padded.shape[0], -1))
    return jnp.stack(windows)


def forward_conv(values, weight):
    channels_local, frames, height, breadth = values.shape
    positions = frames * height * breadth
    rimmed = with_rims(values)
    own_patches = collect(pad_columns(rimmed), frames, height, breadth, False)
    flat_own = own_patches.reshape(-1, positions)
    flat_weight = weight.reshape(-1, weight.shape[2])
    summed = lax.psum_scatter(
        lax.dot_general(
            flat_weight, flat_own, (((0,), (0,)), ((), ())), preferred_element_type=jnp.float32
        ),
        "chan",
        scatter_dimension=0,
        tiled=True,
    )
    return (summed, own_patches)


def normalize(summed):
    grouped = summed.reshape(summed.shape[0] // (C // GROUPS), -1)
    members = grouped.shape[1] * lax.axis_size("frame") * lax.axis_size("row")
    totals = lax.psum(jnp.sum(grouped, axis=1), ("frame", "row"))
    average = totals / members
    centered = grouped - average[:, None]
    variance = lax.psum(jnp.sum(centered * centered, axis=1), ("frame", "row")) / members
    inv_scale = lax.rsqrt(variance + EPSILON)
    return ((centered * inv_scale[:, None]).reshape(summed.shape), inv_scale)


def norm_back(grad_norm, normed, inv_scale):
    grouped_grad = grad_norm.reshape(inv_scale.shape[0], -1)
    grouped_norm = normed.reshape(inv_scale.shape[0], -1)
    members = grouped_grad.shape[1] * lax.axis_size("frame") * lax.axis_size("row")
    first_sum, second_sum = lax.psum(
        (jnp.sum(grouped_grad, axis=1), jnp.sum(grouped_grad * grouped_norm, axis=1)),
        ("frame", "row"),
    )
    adjusted = (
        grouped_grad
        - (first_sum / members)[:, None]
        - grouped_norm * (second_sum / members)[:, None]
    )
    return (adjusted * inv_scale[:, None]).reshape(grad_norm.shape)


def back_conv(grads, own_patches, weight):
    channels_local, frames, height, breadth = grads.shape
    positions = frames * height * breadth
    flat_own = own_patches.reshape(-1, positions)
    rimmed = with_rims(grads)
    portion = lax.all_gather(rimmed, "chan", axis=0, tiled=True)
    members = portion.shape[0]
    interior = portion[:, 1:-1, 1:-1, :].reshape(members, -1)
    shifted = collect(pad_columns(portion), frames, height, breadth, True)
    merged_w = jnp.transpose(weight, (1, 0, 2)).reshape(channels_local, -1)
    back_sum = jnp.dot(merged_w, shifted.reshape(-1, positions), preferred_element_type=jnp.float32)
    increment = lax.dot_general(
        flat_own, interior, (((1,), (1,)), ((), ())), preferred_element_type=jnp.float32
    )
    increment = increment.reshape(27, channels_local, members)
    return (back_sum, increment)


def reduce_weights(weight_grad):
    return lax.psum(weight_grad, ("frame", "row"))


def shards_general(activations, conv_first, conv_second, cotangent):
    layout = activations.shape
    channels_local = layout[0]
    first_sum, first_patches = forward_conv(activations, conv_first)
    first_norm, first_scale = normalize(first_sum)
    first_gate = jax.nn.sigmoid(first_norm)
    hidden = (first_norm * first_gate).astype(jnp.bfloat16).reshape(layout)
    second_sum, second_patches = forward_conv(hidden, conv_second)
    second_norm, second_scale = normalize(second_sum)
    second_gate = jax.nn.sigmoid(second_norm)
    result = (
        (activations.astype(jnp.float32).reshape(channels_local, -1) + second_norm * second_gate)
        .astype(jnp.bfloat16)
        .reshape(layout)
    )
    flat_cot = cotangent.astype(jnp.float32).reshape(channels_local, -1)
    second_dnorm = flat_cot * second_gate * (1.0 + second_norm * (1.0 - second_gate))
    grad_second = (
        norm_back(second_dnorm, second_norm, second_scale).astype(jnp.bfloat16).reshape(layout)
    )
    hidden_grad, second_weight = back_conv(grad_second, second_patches, conv_second)
    second_total = reduce_weights(second_weight)
    first_dnorm = hidden_grad * first_gate * (1.0 + first_norm * (1.0 - first_gate))
    grad_first = (
        norm_back(first_dnorm, first_norm, first_scale).astype(jnp.bfloat16).reshape(layout)
    )
    conv_back, first_weight = back_conv(grad_first, first_patches, conv_first)
    first_total = reduce_weights(first_weight)
    input_grad = (flat_cot + conv_back).astype(jnp.bfloat16).reshape(layout)
    return (result, input_grad, first_total, second_total)


BF16 = jnp.bfloat16
F32 = jnp.float32
LANES = 128
HIGH = lax.Precision.HIGHEST
SIDES = [(slot, side) for slot in range(4) for side in range(2)]


def call(kernel, outs, args, scratch=(), grid=None, specs=None, flops=0, reads=0, grant=16):
    vmem = pl.BlockSpec(memory_space=pltpu.VMEM)
    in_specs = [pl.BlockSpec(memory_space=pltpu.SMEM)] + [vmem] * (len(args) - 1)
    inner, taken = kernel, len(args)
    kernel = lambda where, *refs: inner(where, *refs[: taken - 1][::-1], *refs[taken - 1 :])
    args = (args[0], *args[:0:-1])
    params = dict(vmem_limit_bytes=grant * 1024 * 1024)
    if grid is not None:
        params["dimension_semantics"] = ("arbitrary",) * len(grid)
    extra = {} if grid is None else {"grid": grid}
    return pl.pallas_call(
        kernel,
        out_shape=outs,
        in_specs=in_specs,
        out_specs=[vmem] * len(outs) if specs is None else specs,
        scratch_shapes=list(scratch),
        compiler_params=pltpu.CompilerParams(**params),
        cost_estimate=pl.CostEstimate(flops=flops, bytes_accessed=reads, transcendentals=0),
        **extra,
    )(*args)


def shift(block, step):
    if step == 1:
        return block
    lane = lax.broadcasted_iota(jnp.int32, block.shape, 1)
    if step == 0:
        moved = pltpu.roll(block, 1, 1)
        return jnp.where(lane == 0, jnp.zeros_like(moved), moved)
    moved = pltpu.roll(block, block.shape[1] - 1, 1)
    return jnp.where(lane == block.shape[1] - 1, jnp.zeros_like(moved), moved)


def fill_shifted(shifted, block, channels, frames, mirrored, base=0, stride=None):
    stride = channels if stride is None else stride
    for place in range(frames + 2):
        for side in range(2):
            cells = block(place, side)
            for tap_col in range(3):
                start = (side * 3 + tap_col) * stride + base
                if not isinstance(start, int):
                    start = pl.multiple_of(start, 16)
                lanes = pl.ds(place * LANES, LANES)
                shifted[pl.ds(start, channels), lanes] = shift(cells, 2 - tap_col if mirrored else tap_col)


def neighbour_block(pieces, place, side, frames, where):
    my_frame = where[0]
    if place == 0:
        cells = jnp.where(my_frame == 2, pieces(3, side, frames - 1), pieces(1, side, frames - 1))
        return jnp.where(my_frame > 0, cells, jnp.zeros_like(cells))
    if place == frames + 1:
        cells = jnp.where(my_frame == 1, pieces(3, side, 0), pieces(1, side, 0))
        return jnp.where(my_frame < 3, cells, jnp.zeros_like(cells))
    return pieces(0, side, place - 1)


def pick(refs):
    return lambda slot, side, frame: refs[2 * slot + side][frame]


def other_tap(where, mirrored):
    return 2 * where[1] if mirrored else 2 - 2 * where[1]


def prepare_kernel(where, first, second, behind_first, behind_second):
    for weight, behind in ((first, behind_first), (second, behind_second)):
        for tap_frame in range(3):
            for side in range(2):
                row = other_tap(where, True) if side else 1
                taps = [weight[9 * tap_frame + 3 * row + tap_col] for tap_col in range(3)]
                behind[tap_frame * 2 + side] = jnp.concatenate(taps, axis=1)


def forward_product(where, weight, shifted, parts, scratch, frames):
    channels, wide = weight.shape[1:]
    out = None
    for tap_frame in range(3):
        for side in range(2):
            row = other_tap(where, False) if side else 1
            taps = weight[pl.ds(9 * tap_frame + 3 * row, 3)].reshape(3 * channels, wide)
            window = shifted[
                pl.ds(side * 3 * channels, 3 * channels), pl.ds(tap_frame * LANES, frames * LANES)
            ]
            term = lax.dot_general(
                taps, window, (((0,), (0,)), ((), ())), preferred_element_type=F32
            )
            out = term if out is None else out + term
    scratch[...] = out
    for slot in range(4):
        owner = jnp.bitwise_xor(where[2], slot)
        rows = pl.ds(pl.multiple_of(owner * channels, 16), channels)
        for frame in range(frames):
            cells = scratch[rows, pl.ds(frame * LANES, LANES)]
            parts[slot][frame] = cells.astype(parts[slot].dtype)


def group_total(mixer, sums):
    wide = jnp.broadcast_to(sums, (sums.shape[0], LANES))
    return jnp.dot(mixer, wide, precision=HIGH, preferred_element_type=F32)


def first_kernel(frames, where, weight, *rest):
    pieces, parts, (shifted, total) = rest[:8], rest[8:12], rest[12:]
    block = lambda place, side: neighbour_block(pick(pieces), place, side, frames, where)
    fill_shifted(shifted, block, weight.shape[1], frames, False)
    forward_product(where, weight, shifted, parts, total, frames)


def statistics(sums, mixer, members):
    acc = None
    for block in sums:
        for frame in range(block.shape[0]):
            acc = block[frame] if acc is None else acc + block[frame]
    mean = group_total(mixer, jnp.sum(acc, axis=1, keepdims=True))[:, :1] / members
    acc = None
    for block in sums:
        for frame in range(block.shape[0]):
            centered = block[frame] - mean
            acc = centered * centered if acc is None else acc + centered * centered
    variance = group_total(mixer, jnp.sum(acc, axis=1, keepdims=True))[:, :1] / members
    return mean, lax.rsqrt(variance + EPSILON)


def second_kernel(frames, members, where, weight, mixer, *rest):
    sums, (hidden, norm, scale), parts, (shifted, total) = rest[:8], rest[8:11], rest[11:15], rest[15:]
    mean, inv = statistics(sums, mixer[...], members)
    for slot, side in SIDES:
        for frame in range(frames):
            normed = (sums[2 * slot + side][frame] - mean) * inv
            hidden[slot, side, frame] = (normed * jax.nn.sigmoid(normed)).astype(BF16)
            if slot == 0 and side == 0:
                norm[frame] = normed
    lane = lax.broadcasted_iota(jnp.int32, scale.shape, 1)
    scale[...] = jnp.where(lane == 0, mean, inv)
    at = lambda slot, side, frame: hidden[slot, side, frame]
    block = lambda place, side: neighbour_block(at, place, side, frames, where)
    fill_shifted(shifted, block, mixer.shape[0], frames, False)
    forward_product(where, weight, shifted, parts, total, frames)


def third_kernel(frames, members, where, mixer, *rest):
    sums, given, own, (result, halo, every, grads, norms) = rest[:8], rest[8:16], rest[16], rest[17:]
    mean, inv = statistics(sums, mixer[...], members)
    first = second = None
    for slot, side in SIDES:
        for frame in range(frames):
            normed = (sums[2 * slot + side][frame] - mean) * inv
            gate = jax.nn.sigmoid(normed)
            grad = given[2 * slot + side][frame].astype(F32) * gate * (1.0 + normed * (1.0 - gate))
            first = grad if first is None else first + grad
            second = grad * normed if second is None else second + grad * normed
            norms[slot, side, frame] = normed
            grads[slot, side, frame] = grad
            if slot == 0 and side == 0:
                result[frame] = (own[frame].astype(F32) + normed * gate).astype(BF16)
    first = group_total(mixer[...], jnp.sum(first, axis=1, keepdims=True))[:, :1] / members
    second = group_total(mixer[...], jnp.sum(second, axis=1, keepdims=True))[:, :1] / members
    for slot, side in SIDES:
        for frame in range(frames):
            cells = grads[slot, side, frame] - first - norms[slot, side, frame] * second
            every[slot, side, frame] = (cells * inv).astype(BF16)
    ready = lambda slot, side, frame: every[slot, side, frame]
    for place in range(frames + 2):
        halo[place] = neighbour_block(ready, place, 0, frames, where)


def fourth_kernel(frames, where, weight, norm, *rest):
    halos, (grad, shifted) = rest[:8], rest[8:]
    channels = norm.shape[1]
    for part in range(4):
        owner = jnp.bitwise_xor(where[2], part)
        block = lambda place, side: halos[2 * part + side][place]
        fill_shifted(shifted, block, channels, frames, True, owner * channels, 4 * channels)
    out = back_product(weight, shifted, frames)
    for frame in range(frames):
        normed = norm[frame]
        gate = jax.nn.sigmoid(normed)
        cells = out[:, frame * LANES : (frame + 1) * LANES]
        grad[frame] = (cells * gate * (1.0 + normed * (1.0 - gate))).astype(BF16)


def back_product(weight, shifted, frames):
    depth = weight.shape[2]
    out = None
    for tap_frame in range(3):
        for side in range(2):
            window = shifted[
                pl.ds(side * depth, depth), pl.ds((2 - tap_frame) * LANES, frames * LANES)
            ]
            term = jnp.dot(weight[tap_frame * 2 + side], window, preferred_element_type=F32)
            out = term if out is None else out + term
    return out


def fifth_kernel(frames, members, where, mixer, scale, *rest):
    sums, grads, (out, every) = rest[:8], rest[8:16], rest[16:]
    mean, inv = scale[:, :1], scale[:, 1:2]
    norm = lambda slot, side, frame: (sums[2 * slot + side][frame] - mean) * inv
    first = second = None
    for slot, side in SIDES:
        for frame in range(frames):
            cells = grads[2 * slot + side][frame].astype(F32)
            first = cells if first is None else first + cells
            term = cells * norm(slot, side, frame)
            second = term if second is None else second + term
    first = group_total(mixer[...], jnp.sum(first, axis=1, keepdims=True))[:, :1] / members
    second = group_total(mixer[...], jnp.sum(second, axis=1, keepdims=True))[:, :1] / members
    for slot, side in SIDES:
        for frame in range(frames):
            cells = grads[2 * slot + side][frame].astype(F32)
            cells = cells - first - norm(slot, side, frame) * second
            cells = (cells * inv).astype(BF16)
            every[slot, side, frame] = cells
            if slot in (0, 3) and side == 0:
                out[slot // 3, frame] = cells


def pad_kernel(frames, where, *rest):
    pieces, padded = rest[:8], rest[8]
    fill_padded(padded, pick(pieces), frames, where, pieces[0].shape[1])


def lanes_of(where, slot, frames, frame):
    start = jnp.bitwise_xor(where[0], slot) * frames + frame
    return pl.ds(pl.multiple_of(start * LANES, LANES), LANES)


def fill_padded(padded, inputs, frames, where, channels):
    zeros = jnp.zeros((padded.shape[0], LANES), padded.dtype)
    padded[:, pl.ds(0, LANES)] = zeros
    padded[:, pl.ds(padded.shape[1] - LANES, LANES)] = zeros
    for slot, side in SIDES:
        for frame in range(frames):
            cells = inputs(slot, side, frame)
            for tap_col in range(3):
                rows = pl.ds((side * 3 + tap_col) * channels, channels)
                padded[rows, lanes_of(where, slot, frames, frame + 1)] = shift(cells, tap_col)


def weight_step(grads, frames, where, channels, out, padded, full, ready, sent, finish=None):
    under_rows = -(-4 * channels // LANES) * LANES
    gap = under_rows - 4 * channels
    full[pl.ds(4 * channels, gap), :] = jnp.zeros((gap, full.shape[1]), full.dtype)
    for slot, side in SIDES:
        for frame in range(frames):
            for part in range(4):
                owner = jnp.bitwise_xor(where[2], part)
                rows = pl.ds(pl.multiple_of(side * under_rows + owner * channels, 16), channels)
                full[rows, lanes_of(where, slot, frames, frame)] = grads(slot, side, part, frame)
    copies = []
    for tap_frame in range(3):
        window = padded[:, pl.ds(tap_frame * LANES, full.shape[1])]
        both = lax.dot_general(window, full[...], (((1,), (1,)), ((), ())), preferred_element_type=F32)
        mine, theirs = both[:, : 4 * channels], both[:, under_rows:]
        for tap_col in range(3):
            upper = slice(tap_col * channels, (tap_col + 1) * channels)
            under = slice((3 + tap_col) * channels, (4 + tap_col) * channels)
            ready[tap_frame, 3 + tap_col] = mine[upper] + theirs[under]
            ready[tap_frame, 3 * other_tap(where, False) + tap_col] = mine[under]
            ready[tap_frame, 3 * other_tap(where, True) + tap_col] = theirs[upper]
        copies.append(
            pltpu.make_async_copy(ready.at[tap_frame], out.at[pl.ds(9 * tap_frame, 9)], sent.at[tap_frame])
        )
        copies[-1].start()
    if finish is not None:
        finish()
    for copy in copies:
        copy.wait()


def pad_hidden_kernel(frames, where, hidden, padded):
    inputs = lambda slot, side, frame: hidden[slot, side, frame]
    fill_padded(padded, inputs, frames, where, hidden.shape[3])


def weight_kernel(frames, where, padded, every, *rest):
    own, far, (out, full, ready, sent) = rest[:6], rest[6:12], rest[12:]
    channels = every.shape[3]

    def grads(slot, side, part, frame):
        if part == 0:
            return every[slot, side, frame]
        if slot == 0:
            return own[2 * (part - 1) + side][frame + 1]
        return far[2 * (slot - 1) + side][part - 1, frame]

    weight_step(grads, frames, where, channels, out, padded, full, ready, sent)


def last_kernel(frames, where, weight, cotangent, padded, every, *rest):
    far, (out, back, full, shifted, ready, sent) = rest[:8], rest[8:]
    channels = weight.shape[1]

    def grads(slot, side, part, frame):
        if part == 0:
            return every[slot, side, frame]
        return far[2 * slot + side][part - 1, frame]

    def finish():
        for part in range(4):
            pieces = lambda slot, side, frame: grads(slot, side, part, frame)
            block = lambda place, side: neighbour_block(pieces, place, side, frames, where)
            owner = jnp.bitwise_xor(where[2], part)
            fill_shifted(shifted, block, channels, frames, True, owner * channels, 4 * channels)
        grown = back_product(weight, shifted, frames)
        for frame in range(frames):
            cells = cotangent[frame].astype(F32) + grown[:, frame * LANES : (frame + 1) * LANES]
            back[frame] = cells.astype(BF16)

    weight_step(grads, frames, where, channels, out, padded, full, ready, sent, finish)


def swap(values):
    return lax.ppermute(values, "row", [(0, 1), (1, 0)])


def hop(values, axis, step):
    return lax.ppermute(values, axis, [(i, i ^ step) for i in range(4)])


def over_channels(parts):
    return parts[0] + sum(hop(parts[k], "chan", k).astype(F32) for k in range(1, 4))


def hops(values):
    return [hop(values, "frame", k) for k in range(1, 4)]


def with_sides(pieces):
    return [values for piece in pieces for values in (piece, swap(piece))]


def around(values):
    return with_sides([values] + hops(values))


def shards_paired(activations, conv_first, conv_second, cotangent):
    channels, frames = activations.shape[:2]
    cells = frames * LANES
    count = lax.axis_size("frame")
    wide = 4 * channels
    members = (C // GROUPS) * cells * count * 2
    my_frame, my_row, place = (lax.axis_index(a) for a in ("frame", "row", "chan"))
    where = jnp.stack([my_frame, my_row, place]).astype(jnp.int32)
    group = np.arange(channels) // (C // GROUPS)
    mixer = jnp.asarray((group[:, None] == group[None, :]).astype(np.float32))
    conv_cost = dict(flops=2 * channels * wide * 18 * cells, reads=18 * channels * wide * 2)

    block = (frames, channels, LANES)
    sums_shape = jax.ShapeDtypeStruct(block, F32)
    cells_shape = jax.ShapeDtypeStruct(block, BF16)
    parts_shape = [sums_shape] + [jax.ShapeDtypeStruct(block, LINK)] * 3
    span = (frames + 2) * LANES
    shifted = pltpu.VMEM((6 * channels, span), BF16)
    wide_shifted = pltpu.VMEM((6 * wide, span), BF16)
    total = pltpu.VMEM((wide, cells), F32)

    by_frame = lambda values: values.transpose(1, 2, 0, 3).reshape(block)
    restore = lambda values: values.reshape(frames, 1, channels, LANES).transpose(2, 0, 1, 3)
    inputs, given = by_frame(activations), by_frame(cotangent)
    behind_shape = jax.ShapeDtypeStruct((6, channels, 3 * wide), BF16)
    prepared = call(
        prepare_kernel, [behind_shape, behind_shape], (where, conv_first, conv_second), reads=6000000
    )
    near, (behind_first, behind_second) = lax.optimization_barrier((hops(inputs), prepared))
    every_input = with_sides([inputs] + near)
    parts = call(
        functools.partial(first_kernel, frames), parts_shape,
        (where, conv_first, *every_input), (shifted, total), **conv_cost,
    )
    given, parts = lax.optimization_barrier((given, parts))
    near, sums = lax.optimization_barrier((hops(given), over_channels(parts)))
    every_given = with_sides([given] + near)
    first_sums = around(sums)
    hidden, norm, scale, *parts = call(
        functools.partial(second_kernel, frames, members),
        [
            jax.ShapeDtypeStruct((count, 2, *block), BF16),
            sums_shape,
            jax.ShapeDtypeStruct((channels, LANES), F32),
            *parts_shape,
        ],
        (where, conv_second, mixer, *first_sums), (shifted, total), **conv_cost,
    )
    padded_shape = jax.ShapeDtypeStruct((6 * channels, (frames * count + 2) * LANES), BF16)
    (padded_inputs,) = call(
        functools.partial(pad_kernel, frames), [padded_shape], (where, *every_input), reads=2000000
    )
    far = [hop(parts[k], "chan", k) for k in range(1, 4)]
    far, padded_inputs = lax.optimization_barrier((far, padded_inputs))
    second_sums = around(parts[0] + sum(values.astype(F32) for values in far))
    every_shape = jax.ShapeDtypeStruct((count, 2, *block), BF16)
    result, halo, every_second = call(
        functools.partial(third_kernel, frames, members),
        [cells_shape, jax.ShapeDtypeStruct((frames + 2, channels, LANES), BF16), every_shape],
        (where, mixer, *second_sums, *every_given, inputs),
        (pltpu.VMEM((4, 2, *block), F32), pltpu.VMEM((4, 2, *block), F32)), grant=24,
    )
    (padded_hidden,) = call(
        functools.partial(pad_hidden_kernel, frames), [padded_shape], (where, hidden), reads=2000000
    )
    far = [hop(halo, "chan", k) for k in range(1, 4)]
    far, padded_hidden = lax.optimization_barrier((far, padded_hidden))
    halos = [halo] + far
    sides = with_sides(halos)
    (grad,) = call(
        functools.partial(fourth_kernel, frames), [cells_shape],
        (where, behind_second, norm, *sides), (wide_shifted,), **conv_cost,
    )
    grad_first, every_first = call(
        functools.partial(fifth_kernel, frames, members),
        [jax.ShapeDtypeStruct((2, *block), BF16), every_shape],
        (where, mixer, scale, *first_sums, *around(grad)),
    )
    rest = jnp.stack([values[1:-1] for values in halos[1:]])
    rest, grad_first = lax.optimization_barrier((rest, grad_first))
    far = [hop(grad_first, "chan", k) for k in range(1, 4)]
    far = [jnp.stack([values[k] for values in far]) for k in range(2)]
    near, _ = lax.optimization_barrier((hops(rest), far))
    full = pltpu.VMEM((-(-wide // LANES) * LANES + wide, cells * count), BF16)
    grad_shape = jax.ShapeDtypeStruct((27, channels, wide), F32)
    grad_spec = pl.BlockSpec(memory_space=pl.ANY)
    staging = (pltpu.VMEM((3, 9, channels, wide), F32), pltpu.SemaphoreType.DMA((3,)))
    grad_cost = dict(flops=2 * 18 * channels * wide * cells * count * 2, reads=8000000)
    (second_grad,) = call(
        functools.partial(weight_kernel, frames), [grad_shape],
        (where, padded_hidden, every_second, *sides[2:], *with_sides(near)), (full, *staging),
        specs=[grad_spec], grant=32, **grad_cost,
    )
    near, second_grad = lax.optimization_barrier(([hop(far[0], "frame", k) for k in (1, 2)], second_grad))
    first_grad, input_grad = call(
        functools.partial(last_kernel, frames), [grad_shape, cells_shape],
        (where, behind_first, given, padded_inputs, every_first, *with_sides([far[0], *near, far[1]])),
        (full, wide_shifted, *staging),
        specs=[grad_spec, pl.BlockSpec(memory_space=pltpu.VMEM)], grant=32, **grad_cost,
    )
    return (restore(result), restore(input_grad), first_grad, second_grad)


def paired(mesh):
    return mesh.shape["frame"] == 4 and mesh.shape["row"] == 2 and mesh.shape["chan"] == 4


def solution(mesh):
    return jax.shard_map(
        shards_paired if paired(mesh) else shards_general,
        mesh=mesh,
        in_specs=(
            P("chan", "frame", "row", None),
            P(None, "chan", None),
            P(None, "chan", None),
            P("chan", "frame", "row", None),
        ),
        out_specs=(
            P("chan", "frame", "row", None),
            P("chan", "frame", "row", None),
            P(None, "chan", None),
            P(None, "chan", None),
        ),
        check_vma=False,
    )
```

```python
import functools

import jax
import jax.numpy as jnp
import numpy as np
from jax import lax
from jax.experimental import pallas as pl
from jax.experimental.pallas import tpu as pltpu
from jax.sharding import PartitionSpec as P

C = 320
GROUPS = 32


EPSILON = 1e-05
LINK = jnp.bfloat16


def with_halo(cells, sides, width):
    for axis, dim in sides:
        count = lax.axis_size(axis)
        ends = count - 1
        head = lax.slice_in_dim(cells, 0, width, axis=dim)
        tail = lax.slice_in_dim(cells, cells.shape[dim] - width, cells.shape[dim], axis=dim)
        cells = jnp.concatenate(
            [
                lax.ppermute(tail, axis, [(i, (i + 1) % count) for i in range(ends)]),
                cells,
                lax.ppermute(head, axis, [((i + 1) % count, i) for i in range(ends)]),
            ],
            axis=dim,
        )
    return cells


def pad_columns(values):
    return jnp.pad(values, ((0, 0), (0, 0), (0, 0), (1, 1)))


def with_rims(values):
    return with_halo(values, (("frame", 1), ("row", 2)), 1)


def collect(padded, frames, height, breadth, mirrored):
    windows = []
    for tap_frame in range(3):
        for tap_row in range(3):
            for tap_col in range(3):
                if mirrored:
                    anchor = (2 - tap_frame, 2 - tap_row, 2 - tap_col)
                else:
                    anchor = (tap_frame, tap_row, tap_col)
                window = padded[
                    :,
                    anchor[0] : anchor[0] + frames,
                    anchor[1] : anchor[1] + height,
                    anchor[2] : anchor[2] + breadth,
                ]
                windows.append(window.reshape(padded.shape[0], -1))
    return jnp.stack(windows)


def forward_conv(values, weight):
    channels_local, frames, height, breadth = values.shape
    positions = frames * height * breadth
    rimmed = with_rims(values)
    own_patches = collect(pad_columns(rimmed), frames, height, breadth, False)
    flat_own = own_patches.reshape(-1, positions)
    flat_weight = weight.reshape(-1, weight.shape[2])
    summed = lax.psum_scatter(
        lax.dot_general(
            flat_weight, flat_own, (((0,), (0,)), ((), ())), preferred_element_type=jnp.float32
        ),
        "chan",
        scatter_dimension=0,
        tiled=True,
    )
    return (summed, own_patches)


def normalize(summed):
    grouped = summed.reshape(summed.shape[0] // (C // GROUPS), -1)
    members = grouped.shape[1] * lax.axis_size("frame") * lax.axis_size("row")
    totals = lax.psum(jnp.sum(grouped, axis=1), ("frame", "row"))
    average = totals / members
    centered = grouped - average[:, None]
    variance = lax.psum(jnp.sum(centered * centered, axis=1), ("frame", "row")) / members
    inv_scale = lax.rsqrt(variance + EPSILON)
    return ((centered * inv_scale[:, None]).reshape(summed.shape), inv_scale)


def norm_back(grad_norm, normed, inv_scale):
    grouped_grad = grad_norm.reshape(inv_scale.shape[0], -1)
    grouped_norm = normed.reshape(inv_scale.shape[0], -1)
    members = grouped_grad.shape[1] * lax.axis_size("frame") * lax.axis_size("row")
    first_sum, second_sum = lax.psum(
        (jnp.sum(grouped_grad, axis=1), jnp.sum(grouped_grad * grouped_norm, axis=1)),
        ("frame", "row"),
    )
    adjusted = (
        grouped_grad
        - (first_sum / members)[:, None]
        - grouped_norm * (second_sum / members)[:, None]
    )
    return (adjusted * inv_scale[:, None]).reshape(grad_norm.shape)


def back_conv(grads, own_patches, weight):
    channels_local, frames, height, breadth = grads.shape
    positions = frames * height * breadth
    flat_own = own_patches.reshape(-1, positions)
    rimmed = with_rims(grads)
    portion = lax.all_gather(rimmed, "chan", axis=0, tiled=True)
    members = portion.shape[0]
    interior = portion[:, 1:-1, 1:-1, :].reshape(members, -1)
    shifted = collect(pad_columns(portion), frames, height, breadth, True)
    merged_w = jnp.transpose(weight, (1, 0, 2)).reshape(channels_local, -1)
    back_sum = jnp.dot(merged_w, shifted.reshape(-1, positions), preferred_element_type=jnp.float32)
    increment = lax.dot_general(
        flat_own, interior, (((1,), (1,)), ((), ())), preferred_element_type=jnp.float32
    )
    increment = increment.reshape(27, channels_local, members)
    return (back_sum, increment)


def reduce_weights(weight_grad):
    return lax.psum(weight_grad, ("frame", "row"))


def shards_general(activations, conv_first, conv_second, cotangent):
    layout = activations.shape
    channels_local = layout[0]
    first_sum, first_patches = forward_conv(activations, conv_first)
    first_norm, first_scale = normalize(first_sum)
    first_gate = jax.nn.sigmoid(first_norm)
    hidden = (first_norm * first_gate).astype(jnp.bfloat16).reshape(layout)
    second_sum, second_patches = forward_conv(hidden, conv_second)
    second_norm, second_scale = normalize(second_sum)
    second_gate = jax.nn.sigmoid(second_norm)
    result = (
        (activations.astype(jnp.float32).reshape(channels_local, -1) + second_norm * second_gate)
        .astype(jnp.bfloat16)
        .reshape(layout)
    )
    flat_cot = cotangent.astype(jnp.float32).reshape(channels_local, -1)
    second_dnorm = flat_cot * second_gate * (1.0 + second_norm * (1.0 - second_gate))
    grad_second = (
        norm_back(second_dnorm, second_norm, second_scale).astype(jnp.bfloat16).reshape(layout)
    )
    hidden_grad, second_weight = back_conv(grad_second, second_patches, conv_second)
    second_total = reduce_weights(second_weight)
    first_dnorm = hidden_grad * first_gate * (1.0 + first_norm * (1.0 - first_gate))
    grad_first = (
        norm_back(first_dnorm, first_norm, first_scale).astype(jnp.bfloat16).reshape(layout)
    )
    conv_back, first_weight = back_conv(grad_first, first_patches, conv_first)
    first_total = reduce_weights(first_weight)
    input_grad = (flat_cot + conv_back).astype(jnp.bfloat16).reshape(layout)
    return (result, input_grad, first_total, second_total)


BF16 = jnp.bfloat16
F32 = jnp.float32
LANES = 128
HIGH = lax.Precision.HIGHEST
SIDES = [(slot, side) for slot in range(4) for side in range(2)]


def call(kernel, outs, args, scratch=(), grid=None, specs=None, flops=0, reads=0, grant=16):
    vmem = pl.BlockSpec(memory_space=pltpu.VMEM)
    in_specs = [pl.BlockSpec(memory_space=pltpu.SMEM)] + [vmem] * (len(args) - 1)
    inner, taken = kernel, len(args)
    kernel = lambda where, *refs: inner(where, *refs[: taken - 1][::-1], *refs[taken - 1 :])
    args = (args[0], *args[:0:-1])
    params = dict(vmem_limit_bytes=grant * 1024 * 1024)
    if grid is not None:
        params["dimension_semantics"] = ("arbitrary",) * len(grid)
    extra = {} if grid is None else {"grid": grid}
    return pl.pallas_call(
        kernel,
        out_shape=outs,
        in_specs=in_specs,
        out_specs=[vmem] * len(outs) if specs is None else specs,
        scratch_shapes=list(scratch),
        compiler_params=pltpu.CompilerParams(**params),
        cost_estimate=pl.CostEstimate(flops=flops, bytes_accessed=reads, transcendentals=0),
        **extra,
    )(*args)


def shift(block, step):
    if step == 1:
        return block
    lane = lax.broadcasted_iota(jnp.int32, block.shape, 1)
    if step == 0:
        moved = pltpu.roll(block, 1, 1)
        return jnp.where(lane == 0, jnp.zeros_like(moved), moved)
    moved = pltpu.roll(block, block.shape[1] - 1, 1)
    return jnp.where(lane == block.shape[1] - 1, jnp.zeros_like(moved), moved)


def fill_shifted(shifted, block, channels, frames, mirrored, base=0, stride=None):
    stride = channels if stride is None else stride
    for place in range(frames + 2):
        for side in range(2):
            cells = block(place, side)
            for tap_col in range(3):
                start = (side * 3 + tap_col) * stride + base
                if not isinstance(start, int):
                    start = pl.multiple_of(start, 16)
                lanes = pl.ds(place * LANES, LANES)
                shifted[pl.ds(start, channels), lanes] = shift(cells, 2 - tap_col if mirrored else tap_col)


def neighbour_block(pieces, place, side, frames, where):
    my_frame = where[0]
    if place == 0:
        cells = jnp.where(my_frame == 2, pieces(3, side, frames - 1), pieces(1, side, frames - 1))
        return jnp.where(my_frame > 0, cells, jnp.zeros_like(cells))
    if place == frames + 1:
        cells = jnp.where(my_frame == 1, pieces(3, side, 0), pieces(1, side, 0))
        return jnp.where(my_frame < 3, cells, jnp.zeros_like(cells))
    return pieces(0, side, place - 1)


def pick(refs):
    return lambda slot, side, frame: refs[2 * slot + side][frame]


def other_tap(where, mirrored):
    return 2 * where[1] if mirrored else 2 - 2 * where[1]


def prepare_kernel(where, first, second, behind_first, behind_second):
    for weight, behind in ((first, behind_first), (second, behind_second)):
        for tap_frame in range(3):
            for side in range(2):
                row = other_tap(where, True) if side else 1
                taps = [weight[9 * tap_frame + 3 * row + tap_col] for tap_col in range(3)]
                behind[tap_frame * 2 + side] = jnp.concatenate(taps, axis=1)


def forward_product(where, weight, shifted, parts, scratch, frames):
    channels, wide = weight.shape[1:]
    out = None
    for tap_frame in range(3):
        for side in range(2):
            row = other_tap(where, False) if side else 1
            taps = weight[pl.ds(9 * tap_frame + 3 * row, 3)].reshape(3 * channels, wide)
            window = shifted[
                pl.ds(side * 3 * channels, 3 * channels), pl.ds(tap_frame * LANES, frames * LANES)
            ]
            term = lax.dot_general(
                taps, window, (((0,), (0,)), ((), ())), preferred_element_type=F32
            )
            out = term if out is None else out + term
    scratch[...] = out
    for slot in range(4):
        owner = jnp.bitwise_xor(where[2], slot)
        rows = pl.ds(pl.multiple_of(owner * channels, 16), channels)
        for frame in range(frames):
            cells = scratch[rows, pl.ds(frame * LANES, LANES)]
            parts[slot][frame] = cells.astype(parts[slot].dtype)


def group_total(mixer, sums):
    wide = jnp.broadcast_to(sums, (sums.shape[0], LANES))
    return jnp.dot(mixer, wide, precision=HIGH, preferred_element_type=F32)


def first_kernel(frames, where, weight, *rest):
    pieces, parts, (shifted, total) = rest[:8], rest[8:12], rest[12:]
    block = lambda place, side: neighbour_block(pick(pieces), place, side, frames, where)
    fill_shifted(shifted, block, weight.shape[1], frames, False)
    forward_product(where, weight, shifted, parts, total, frames)


def statistics(sums, mixer, members):
    acc = None
    for block in sums:
        for frame in range(block.shape[0]):
            cells = block[frame].astype(F32)
            acc = cells if acc is None else acc + cells
    mean = group_total(mixer, jnp.sum(acc, axis=1, keepdims=True))[:, :1] / members
    acc = None
    for block in sums:
        for frame in range(block.shape[0]):
            centered = block[frame].astype(F32) - mean
            acc = centered * centered if acc is None else acc + centered * centered
    variance = group_total(mixer, jnp.sum(acc, axis=1, keepdims=True))[:, :1] / members
    return mean, lax.rsqrt(variance + EPSILON)


def second_kernel(frames, members, where, weight, mixer, *rest):
    sums, (hidden, norm, scale), parts, (shifted, total) = rest[:8], rest[8:11], rest[11:15], rest[15:]
    mean, inv = statistics(sums, mixer[...], members)
    for slot, side in SIDES:
        for frame in range(frames):
            normed = (sums[2 * slot + side][frame] - mean) * inv
            hidden[slot, side, frame] = (normed * jax.nn.sigmoid(normed)).astype(BF16)
            if slot == 0 and side == 0:
                norm[frame] = normed
    lane = lax.broadcasted_iota(jnp.int32, scale.shape, 1)
    scale[...] = jnp.where(lane == 0, mean, inv)
    at = lambda slot, side, frame: hidden[slot, side, frame]
    block = lambda place, side: neighbour_block(at, place, side, frames, where)
    fill_shifted(shifted, block, mixer.shape[0], frames, False)
    forward_product(where, weight, shifted, parts, total, frames)


def third_kernel(frames, members, where, mixer, *rest):
    sums, given, own, (result, halo, every, grads, norms) = rest[:8], rest[8:16], rest[16], rest[17:]
    mean, inv = statistics(sums, mixer[...], members)
    first = second = None
    for slot, side in SIDES:
        for frame in range(frames):
            normed = (sums[2 * slot + side][frame].astype(F32) - mean) * inv
            gate = jax.nn.sigmoid(normed)
            grad = given[2 * slot + side][frame].astype(F32) * gate * (1.0 + normed * (1.0 - gate))
            first = grad if first is None else first + grad
            second = grad * normed if second is None else second + grad * normed
            norms[slot, side, frame] = normed
            grads[slot, side, frame] = grad
            if slot == 0 and side == 0:
                result[frame] = (own[frame].astype(F32) + normed * gate).astype(BF16)
    first = group_total(mixer[...], jnp.sum(first, axis=1, keepdims=True))[:, :1] / members
    second = group_total(mixer[...], jnp.sum(second, axis=1, keepdims=True))[:, :1] / members
    for slot, side in SIDES:
        for frame in range(frames):
            cells = grads[slot, side, frame] - first - norms[slot, side, frame] * second
            every[slot, side, frame] = (cells * inv).astype(BF16)
    ready = lambda slot, side, frame: every[slot, side, frame]
    for place in range(frames + 2):
        halo[place] = neighbour_block(ready, place, 0, frames, where)


def fourth_kernel(frames, where, weight, norm, *rest):
    halos, (grad, shifted) = rest[:8], rest[8:]
    channels = norm.shape[1]
    for part in range(4):
        owner = jnp.bitwise_xor(where[2], part)
        block = lambda place, side: halos[2 * part + side][place]
        fill_shifted(shifted, block, channels, frames, True, owner * channels, 4 * channels)
    out = back_product(weight, shifted, frames)
    for frame in range(frames):
        normed = norm[frame]
        gate = jax.nn.sigmoid(normed)
        cells = out[:, frame * LANES : (frame + 1) * LANES]
        grad[frame] = (cells * gate * (1.0 + normed * (1.0 - gate))).astype(BF16)


def back_product(weight, shifted, frames):
    depth = weight.shape[2]
    out = None
    for tap_frame in range(3):
        for side in range(2):
            window = shifted[
                pl.ds(side * depth, depth), pl.ds((2 - tap_frame) * LANES, frames * LANES)
            ]
            term = jnp.dot(weight[tap_frame * 2 + side], window, preferred_element_type=F32)
            out = term if out is None else out + term
    return out


def fifth_kernel(frames, members, where, mixer, scale, *rest):
    sums, grads, (out, every) = rest[:8], rest[8:16], rest[16:]
    mean, inv = scale[:, :1], scale[:, 1:2]
    norm = lambda slot, side, frame: (sums[2 * slot + side][frame] - mean) * inv
    first = second = None
    for slot, side in SIDES:
        for frame in range(frames):
            cells = grads[2 * slot + side][frame].astype(F32)
            first = cells if first is None else first + cells
            term = cells * norm(slot, side, frame)
            second = term if second is None else second + term
    first = group_total(mixer[...], jnp.sum(first, axis=1, keepdims=True))[:, :1] / members
    second = group_total(mixer[...], jnp.sum(second, axis=1, keepdims=True))[:, :1] / members
    for slot, side in SIDES:
        for frame in range(frames):
            cells = grads[2 * slot + side][frame].astype(F32)
            cells = cells - first - norm(slot, side, frame) * second
            cells = (cells * inv).astype(BF16)
            every[slot, side, frame] = cells
            if slot in (0, 3) and side == 0:
                out[slot // 3, frame] = cells


def pad_kernel(frames, where, *rest):
    pieces, padded = rest[:8], rest[8]
    fill_padded(padded, pick(pieces), frames, where, pieces[0].shape[1])


def lanes_of(where, slot, frames, frame):
    start = jnp.bitwise_xor(where[0], slot) * frames + frame
    return pl.ds(pl.multiple_of(start * LANES, LANES), LANES)


def fill_padded(padded, inputs, frames, where, channels):
    zeros = jnp.zeros((padded.shape[0], LANES), padded.dtype)
    padded[:, pl.ds(0, LANES)] = zeros
    padded[:, pl.ds(padded.shape[1] - LANES, LANES)] = zeros
    for slot, side in SIDES:
        for frame in range(frames):
            cells = inputs(slot, side, frame)
            for tap_col in range(3):
                rows = pl.ds((side * 3 + tap_col) * channels, channels)
                padded[rows, lanes_of(where, slot, frames, frame + 1)] = shift(cells, tap_col)


def weight_step(grads, frames, where, channels, out, padded, full, ready, sent, finish=None):
    under_rows = -(-4 * channels // LANES) * LANES
    gap = under_rows - 4 * channels
    full[pl.ds(4 * channels, gap), :] = jnp.zeros((gap, full.shape[1]), full.dtype)
    for slot, side in SIDES:
        for frame in range(frames):
            for part in range(4):
                owner = jnp.bitwise_xor(where[2], part)
                rows = pl.ds(pl.multiple_of(side * under_rows + owner * channels, 16), channels)
                full[rows, lanes_of(where, slot, frames, frame)] = grads(slot, side, part, frame)
    copies = []
    for tap_frame in range(3):
        window = padded[:, pl.ds(tap_frame * LANES, full.shape[1])]
        both = lax.dot_general(window, full[...], (((1,), (1,)), ((), ())), preferred_element_type=F32)
        mine, theirs = both[:, : 4 * channels], both[:, under_rows:]
        for tap_col in range(3):
            upper = slice(tap_col * channels, (tap_col + 1) * channels)
            under = slice((3 + tap_col) * channels, (4 + tap_col) * channels)
            ready[tap_frame, 3 + tap_col] = mine[upper] + theirs[under]
            ready[tap_frame, 3 * other_tap(where, False) + tap_col] = mine[under]
            ready[tap_frame, 3 * other_tap(where, True) + tap_col] = theirs[upper]
        copies.append(
            pltpu.make_async_copy(ready.at[tap_frame], out.at[pl.ds(9 * tap_frame, 9)], sent.at[tap_frame])
        )
        copies[-1].start()
    if finish is not None:
        finish()
    for copy in copies:
        copy.wait()


def pad_hidden_kernel(frames, where, hidden, padded):
    inputs = lambda slot, side, frame: hidden[slot, side, frame]
    fill_padded(padded, inputs, frames, where, hidden.shape[3])


def weight_kernel(frames, where, padded, every, *rest):
    own, far, (out, full, ready, sent) = rest[:6], rest[6:12], rest[12:]
    channels = every.shape[3]

    def grads(slot, side, part, frame):
        if part == 0:
            return every[slot, side, frame]
        if slot == 0:
            return own[2 * (part - 1) + side][frame + 1]
        return far[2 * (slot - 1) + side][part - 1, frame]

    weight_step(grads, frames, where, channels, out, padded, full, ready, sent)


def last_kernel(frames, where, weight, cotangent, padded, every, *rest):
    far, (out, back, full, shifted, ready, sent) = rest[:8], rest[8:]
    channels = weight.shape[1]

    def grads(slot, side, part, frame):
        if part == 0:
            return every[slot, side, frame]
        return far[2 * slot + side][part - 1, frame]

    def finish():
        for part in range(4):
            pieces = lambda slot, side, frame: grads(slot, side, part, frame)
            block = lambda place, side: neighbour_block(pieces, place, side, frames, where)
            owner = jnp.bitwise_xor(where[2], part)
            fill_shifted(shifted, block, channels, frames, True, owner * channels, 4 * channels)
        grown = back_product(weight, shifted, frames)
        for frame in range(frames):
            cells = cotangent[frame].astype(F32) + grown[:, frame * LANES : (frame + 1) * LANES]
            back[frame] = cells.astype(BF16)

    weight_step(grads, frames, where, channels, out, padded, full, ready, sent, finish)


def swap(values):
    return lax.ppermute(values, "row", [(0, 1), (1, 0)])


def hop(values, axis, step):
    return lax.ppermute(values, axis, [(i, i ^ step) for i in range(4)])


def over_channels(parts):
    return parts[0] + sum(hop(parts[k], "chan", k).astype(F32) for k in range(1, 4))


def hops(values):
    return [hop(values, "frame", k) for k in range(1, 4)]


def with_sides(pieces):
    return [values for piece in pieces for values in (piece, swap(piece))]


def around(values):
    return with_sides([values] + hops(values))


def shards_paired(activations, conv_first, conv_second, cotangent):
    channels, frames = activations.shape[:2]
    cells = frames * LANES
    count = lax.axis_size("frame")
    wide = 4 * channels
    members = (C // GROUPS) * cells * count * 2
    my_frame, my_row, place = (lax.axis_index(a) for a in ("frame", "row", "chan"))
    where = jnp.stack([my_frame, my_row, place]).astype(jnp.int32)
    group = np.arange(channels) // (C // GROUPS)
    mixer = jnp.asarray((group[:, None] == group[None, :]).astype(np.float32))
    conv_cost = dict(flops=2 * channels * wide * 18 * cells, reads=18 * channels * wide * 2)

    block = (frames, channels, LANES)
    sums_shape = jax.ShapeDtypeStruct(block, F32)
    cells_shape = jax.ShapeDtypeStruct(block, BF16)
    parts_shape = [sums_shape] + [jax.ShapeDtypeStruct(block, LINK)] * 3
    span = (frames + 2) * LANES
    shifted = pltpu.VMEM((6 * channels, span), BF16)
    wide_shifted = pltpu.VMEM((6 * wide, span), BF16)
    total = pltpu.VMEM((wide, cells), F32)

    by_frame = lambda values: values.transpose(1, 2, 0, 3).reshape(block)
    restore = lambda values: values.reshape(frames, 1, channels, LANES).transpose(2, 0, 1, 3)
    inputs, given = by_frame(activations), by_frame(cotangent)
    behind_shape = jax.ShapeDtypeStruct((6, channels, 3 * wide), BF16)
    prepared = call(
        prepare_kernel, [behind_shape, behind_shape], (where, conv_first, conv_second), reads=6000000
    )
    near, (behind_first, behind_second) = lax.optimization_barrier((hops(inputs), prepared))
    every_input = with_sides([inputs] + near)
    parts = call(
        functools.partial(first_kernel, frames), parts_shape,
        (where, conv_first, *every_input), (shifted, total), **conv_cost,
    )
    given, parts = lax.optimization_barrier((given, parts))
    near, sums = lax.optimization_barrier((hops(given), over_channels(parts)))
    every_given = with_sides([given] + near)
    first_sums = around(sums)
    hidden, norm, scale, *parts = call(
        functools.partial(second_kernel, frames, members),
        [
            jax.ShapeDtypeStruct((count, 2, *block), BF16),
            sums_shape,
            jax.ShapeDtypeStruct((channels, LANES), F32),
            *parts_shape,
        ],
        (where, conv_second, mixer, *first_sums), (shifted, total), **conv_cost,
    )
    padded_shape = jax.ShapeDtypeStruct((6 * channels, (frames * count + 2) * LANES), BF16)
    (padded_inputs,) = call(
        functools.partial(pad_kernel, frames), [padded_shape], (where, *every_input), reads=2000000
    )
    far = [hop(parts[k], "chan", k) for k in range(1, 4)]
    far, padded_inputs = lax.optimization_barrier((far, padded_inputs))
    sums = parts[0] + sum(values.astype(F32) for values in far)
    second_sums = [sums, *around(sums.astype(BF16))[1:]]
    every_shape = jax.ShapeDtypeStruct((count, 2, *block), BF16)
    result, halo, every_second = call(
        functools.partial(third_kernel, frames, members),
        [cells_shape, jax.ShapeDtypeStruct((frames + 2, channels, LANES), BF16), every_shape],
        (where, mixer, *second_sums, *every_given, inputs),
        (pltpu.VMEM((4, 2, *block), F32), pltpu.VMEM((4, 2, *block), F32)), grant=24,
    )
    (padded_hidden,) = call(
        functools.partial(pad_hidden_kernel, frames), [padded_shape], (where, hidden), reads=2000000
    )
    far = [hop(halo, "chan", k) for k in range(1, 4)]
    far, padded_hidden = lax.optimization_barrier((far, padded_hidden))
    halos = [halo] + far
    sides = with_sides(halos)
    (grad,) = call(
        functools.partial(fourth_kernel, frames), [cells_shape],
        (where, behind_second, norm, *sides), (wide_shifted,), **conv_cost,
    )
    grad_first, every_first = call(
        functools.partial(fifth_kernel, frames, members),
        [jax.ShapeDtypeStruct((2, *block), BF16), every_shape],
        (where, mixer, scale, *first_sums, *around(grad)),
    )
    rest = jnp.stack([values[1:-1] for values in halos[1:]])
    rest, grad_first = lax.optimization_barrier((rest, grad_first))
    far = [hop(grad_first, "chan", k) for k in range(1, 4)]
    far = [jnp.stack([values[k] for values in far]) for k in range(2)]
    near, _ = lax.optimization_barrier((hops(rest), far))
    full = pltpu.VMEM((-(-wide // LANES) * LANES + wide, cells * count), BF16)
    grad_shape = jax.ShapeDtypeStruct((27, channels, wide), F32)
    grad_spec = pl.BlockSpec(memory_space=pl.ANY)
    staging = (pltpu.VMEM((3, 9, channels, wide), F32), pltpu.SemaphoreType.DMA((3,)))
    grad_cost = dict(flops=2 * 18 * channels * wide * cells * count * 2, reads=8000000)
    (second_grad,) = call(
        functools.partial(weight_kernel, frames), [grad_shape],
        (where, padded_hidden, every_second, *sides[2:], *with_sides(near)), (full, *staging),
        specs=[grad_spec], grant=32, **grad_cost,
    )
    near, second_grad = lax.optimization_barrier(([hop(far[0], "frame", k) for k in (1, 2)], second_grad))
    first_grad, input_grad = call(
        functools.partial(last_kernel, frames), [grad_shape, cells_shape],
        (where, behind_first, given, padded_inputs, every_first, *with_sides([far[0], *near, far[1]])),
        (full, wide_shifted, *staging),
        specs=[grad_spec, pl.BlockSpec(memory_space=pltpu.VMEM)], grant=32, **grad_cost,
    )
    return (restore(result), restore(input_grad), first_grad, second_grad)


def paired(mesh):
    return mesh.shape["frame"] == 4 and mesh.shape["row"] == 2 and mesh.shape["chan"] == 4


def solution(mesh):
    return jax.shard_map(
        shards_paired if paired(mesh) else shards_general,
        mesh=mesh,
        in_specs=(
            P("chan", "frame", "row", None),
            P(None, "chan", None),
            P(None, "chan", None),
            P("chan", "frame", "row", None),
        ),
        out_specs=(
            P("chan", "frame", "row", None),
            P("chan", "frame", "row", None),
            P(None, "chan", None),
            P(None, "chan", None),
        ),
        check_vma=False,
    )
```

```python
import functools

import jax
import jax.numpy as jnp
import numpy as np
from jax import lax
from jax.experimental import pallas as pl
from jax.experimental.pallas import tpu as pltpu
from jax.sharding import PartitionSpec as P

C = 320
GROUPS = 32


EPSILON = 1e-05
LINK = jnp.bfloat16


def with_halo(cells, sides, width):
    for axis, dim in sides:
        count = lax.axis_size(axis)
        ends = count - 1
        head = lax.slice_in_dim(cells, 0, width, axis=dim)
        tail = lax.slice_in_dim(cells, cells.shape[dim] - width, cells.shape[dim], axis=dim)
        cells = jnp.concatenate(
            [
                lax.ppermute(tail, axis, [(i, (i + 1) % count) for i in range(ends)]),
                cells,
                lax.ppermute(head, axis, [((i + 1) % count, i) for i in range(ends)]),
            ],
            axis=dim,
        )
    return cells


def pad_columns(values):
    return jnp.pad(values, ((0, 0), (0, 0), (0, 0), (1, 1)))


def with_rims(values):
    return with_halo(values, (("frame", 1), ("row", 2)), 1)


def collect(padded, frames, height, breadth, mirrored):
    windows = []
    for tap_frame in range(3):
        for tap_row in range(3):
            for tap_col in range(3):
                if mirrored:
                    anchor = (2 - tap_frame, 2 - tap_row, 2 - tap_col)
                else:
                    anchor = (tap_frame, tap_row, tap_col)
                window = padded[
                    :,
                    anchor[0] : anchor[0] + frames,
                    anchor[1] : anchor[1] + height,
                    anchor[2] : anchor[2] + breadth,
                ]
                windows.append(window.reshape(padded.shape[0], -1))
    return jnp.stack(windows)


def forward_conv(values, weight):
    channels_local, frames, height, breadth = values.shape
    positions = frames * height * breadth
    rimmed = with_rims(values)
    own_patches = collect(pad_columns(rimmed), frames, height, breadth, False)
    flat_own = own_patches.reshape(-1, positions)
    flat_weight = weight.reshape(-1, weight.shape[2])
    summed = lax.psum_scatter(
        lax.dot_general(
            flat_weight, flat_own, (((0,), (0,)), ((), ())), preferred_element_type=jnp.float32
        ),
        "chan",
        scatter_dimension=0,
        tiled=True,
    )
    return (summed, own_patches)


def normalize(summed):
    grouped = summed.reshape(summed.shape[0] // (C // GROUPS), -1)
    members = grouped.shape[1] * lax.axis_size("frame") * lax.axis_size("row")
    totals = lax.psum(jnp.sum(grouped, axis=1), ("frame", "row"))
    average = totals / members
    centered = grouped - average[:, None]
    variance = lax.psum(jnp.sum(centered * centered, axis=1), ("frame", "row")) / members
    inv_scale = lax.rsqrt(variance + EPSILON)
    return ((centered * inv_scale[:, None]).reshape(summed.shape), inv_scale)


def norm_back(grad_norm, normed, inv_scale):
    grouped_grad = grad_norm.reshape(inv_scale.shape[0], -1)
    grouped_norm = normed.reshape(inv_scale.shape[0], -1)
    members = grouped_grad.shape[1] * lax.axis_size("frame") * lax.axis_size("row")
    first_sum, second_sum = lax.psum(
        (jnp.sum(grouped_grad, axis=1), jnp.sum(grouped_grad * grouped_norm, axis=1)),
        ("frame", "row"),
    )
    adjusted = (
        grouped_grad
        - (first_sum / members)[:, None]
        - grouped_norm * (second_sum / members)[:, None]
    )
    return (adjusted * inv_scale[:, None]).reshape(grad_norm.shape)


def back_conv(grads, own_patches, weight):
    channels_local, frames, height, breadth = grads.shape
    positions = frames * height * breadth
    flat_own = own_patches.reshape(-1, positions)
    rimmed = with_rims(grads)
    portion = lax.all_gather(rimmed, "chan", axis=0, tiled=True)
    members = portion.shape[0]
    interior = portion[:, 1:-1, 1:-1, :].reshape(members, -1)
    shifted = collect(pad_columns(portion), frames, height, breadth, True)
    merged_w = jnp.transpose(weight, (1, 0, 2)).reshape(channels_local, -1)
    back_sum = jnp.dot(merged_w, shifted.reshape(-1, positions), preferred_element_type=jnp.float32)
    increment = lax.dot_general(
        flat_own, interior, (((1,), (1,)), ((), ())), preferred_element_type=jnp.float32
    )
    increment = increment.reshape(27, channels_local, members)
    return (back_sum, increment)


def reduce_weights(weight_grad):
    return lax.psum(weight_grad, ("frame", "row"))


def shards_general(activations, conv_first, conv_second, cotangent):
    layout = activations.shape
    channels_local = layout[0]
    first_sum, first_patches = forward_conv(activations, conv_first)
    first_norm, first_scale = normalize(first_sum)
    first_gate = jax.nn.sigmoid(first_norm)
    hidden = (first_norm * first_gate).astype(jnp.bfloat16).reshape(layout)
    second_sum, second_patches = forward_conv(hidden, conv_second)
    second_norm, second_scale = normalize(second_sum)
    second_gate = jax.nn.sigmoid(second_norm)
    result = (
        (activations.astype(jnp.float32).reshape(channels_local, -1) + second_norm * second_gate)
        .astype(jnp.bfloat16)
        .reshape(layout)
    )
    flat_cot = cotangent.astype(jnp.float32).reshape(channels_local, -1)
    second_dnorm = flat_cot * second_gate * (1.0 + second_norm * (1.0 - second_gate))
    grad_second = (
        norm_back(second_dnorm, second_norm, second_scale).astype(jnp.bfloat16).reshape(layout)
    )
    hidden_grad, second_weight = back_conv(grad_second, second_patches, conv_second)
    second_total = reduce_weights(second_weight)
    first_dnorm = hidden_grad * first_gate * (1.0 + first_norm * (1.0 - first_gate))
    grad_first = (
        norm_back(first_dnorm, first_norm, first_scale).astype(jnp.bfloat16).reshape(layout)
    )
    conv_back, first_weight = back_conv(grad_first, first_patches, conv_first)
    first_total = reduce_weights(first_weight)
    input_grad = (flat_cot + conv_back).astype(jnp.bfloat16).reshape(layout)
    return (result, input_grad, first_total, second_total)


BF16 = jnp.bfloat16
F32 = jnp.float32
LANES = 128
HIGH = lax.Precision.HIGHEST
SIDES = [(slot, side) for slot in range(4) for side in range(2)]


def gate_of(values):
    return 0.5 + 0.5 * jnp.tanh(0.5 * values)


def call(kernel, outs, args, scratch=(), grid=None, specs=None, flops=0, reads=0, grant=16):
    vmem = pl.BlockSpec(memory_space=pltpu.VMEM)
    in_specs = [pl.BlockSpec(memory_space=pltpu.SMEM)] + [vmem] * (len(args) - 1)
    inner, taken = kernel, len(args)
    kernel = lambda where, *refs: inner(where, *refs[: taken - 1][::-1], *refs[taken - 1 :])
    args = (args[0], *args[:0:-1])
    params = dict(vmem_limit_bytes=grant * 1024 * 1024)
    if grid is not None:
        params["dimension_semantics"] = ("arbitrary",) * len(grid)
    extra = {} if grid is None else {"grid": grid}
    return pl.pallas_call(
        kernel,
        out_shape=outs,
        in_specs=in_specs,
        out_specs=[vmem] * len(outs) if specs is None else specs,
        scratch_shapes=list(scratch),
        compiler_params=pltpu.CompilerParams(**params),
        cost_estimate=pl.CostEstimate(flops=flops, bytes_accessed=reads, transcendentals=0),
        **extra,
    )(*args)


def shift(block, step):
    if step == 1:
        return block
    lane = lax.broadcasted_iota(jnp.int32, block.shape, 1)
    if step == 0:
        moved = pltpu.roll(block, 1, 1)
        return jnp.where(lane == 0, jnp.zeros_like(moved), moved)
    moved = pltpu.roll(block, block.shape[1] - 1, 1)
    return jnp.where(lane == block.shape[1] - 1, jnp.zeros_like(moved), moved)


def fill_shifted(shifted, block, channels, frames, mirrored, base=0, stride=None):
    stride = channels if stride is None else stride
    for place in range(frames + 2):
        for side in range(2):
            cells = block(place, side)
            for tap_col in range(3):
                start = (side * 3 + tap_col) * stride + base
                if not isinstance(start, int):
                    start = pl.multiple_of(start, 16)
                lanes = pl.ds(place * LANES, LANES)
                shifted[pl.ds(start, channels), lanes] = shift(cells, 2 - tap_col if mirrored else tap_col)


def neighbour_block(pieces, place, side, frames, where):
    my_frame = where[0]
    if place == 0:
        cells = jnp.where(my_frame == 2, pieces(3, side, frames - 1), pieces(1, side, frames - 1))
        return jnp.where(my_frame > 0, cells, jnp.zeros_like(cells))
    if place == frames + 1:
        cells = jnp.where(my_frame == 1, pieces(3, side, 0), pieces(1, side, 0))
        return jnp.where(my_frame < 3, cells, jnp.zeros_like(cells))
    return pieces(0, side, place - 1)


def pick(refs):
    return lambda slot, side, frame: refs[2 * slot + side][frame]


def other_tap(where, mirrored):
    return 2 * where[1] if mirrored else 2 - 2 * where[1]


def prepare_kernel(where, first, second, behind_first, behind_second):
    for weight, behind in ((first, behind_first), (second, behind_second)):
        for tap_frame in range(3):
            for side in range(2):
                row = other_tap(where, True) if side else 1
                taps = [weight[9 * tap_frame + 3 * row + tap_col] for tap_col in range(3)]
                behind[tap_frame * 2 + side] = jnp.concatenate(taps, axis=1)


def forward_product(where, weight, shifted, parts, scratch, frames):
    channels, wide = weight.shape[1:]
    out = None
    for tap_frame in range(3):
        for side in range(2):
            row = other_tap(where, False) if side else 1
            taps = weight[pl.ds(9 * tap_frame + 3 * row, 3)].reshape(3 * channels, wide)
            window = shifted[
                pl.ds(side * 3 * channels, 3 * channels), pl.ds(tap_frame * LANES, frames * LANES)
            ]
            term = lax.dot_general(
                taps, window, (((0,), (0,)), ((), ())), preferred_element_type=F32
            )
            out = term if out is None else out + term
    scratch[...] = out
    for slot in range(4):
        owner = jnp.bitwise_xor(where[2], slot)
        rows = pl.ds(pl.multiple_of(owner * channels, 16), channels)
        for frame in range(frames):
            cells = scratch[rows, pl.ds(frame * LANES, LANES)]
            parts[slot][frame] = cells.astype(parts[slot].dtype)


def group_total(mixer, sums):
    wide = jnp.broadcast_to(sums, (sums.shape[0], LANES))
    return jnp.dot(mixer, wide, precision=HIGH, preferred_element_type=F32)


def first_kernel(frames, where, weight, *rest):
    pieces, parts, (shifted, total) = rest[:8], rest[8:12], rest[12:]
    block = lambda place, side: neighbour_block(pick(pieces), place, side, frames, where)
    fill_shifted(shifted, block, weight.shape[1], frames, False)
    forward_product(where, weight, shifted, parts, total, frames)


def statistics(sums, mixer, members):
    acc = None
    for block in sums:
        for frame in range(block.shape[0]):
            cells = block[frame].astype(F32)
            acc = cells if acc is None else acc + cells
    mean = group_total(mixer, jnp.sum(acc, axis=1, keepdims=True))[:, :1] / members
    acc = None
    for block in sums:
        for frame in range(block.shape[0]):
            centered = block[frame].astype(F32) - mean
            acc = centered * centered if acc is None else acc + centered * centered
    variance = group_total(mixer, jnp.sum(acc, axis=1, keepdims=True))[:, :1] / members
    return mean, lax.rsqrt(variance + EPSILON)


def second_kernel(frames, members, where, weight, mixer, *rest):
    sums, (hidden, norm, scale), parts, (shifted, total) = rest[:8], rest[8:11], rest[11:15], rest[15:]
    mean, inv = statistics(sums, mixer[...], members)
    for slot, side in SIDES:
        for frame in range(frames):
            normed = (sums[2 * slot + side][frame] - mean) * inv
            hidden[slot, side, frame] = (normed * gate_of(normed)).astype(BF16)
            if slot == 0 and side == 0:
                norm[frame] = normed
    lane = lax.broadcasted_iota(jnp.int32, scale.shape, 1)
    scale[...] = jnp.where(lane == 0, mean, inv)
    at = lambda slot, side, frame: hidden[slot, side, frame]
    block = lambda place, side: neighbour_block(at, place, side, frames, where)
    fill_shifted(shifted, block, mixer.shape[0], frames, False)
    forward_product(where, weight, shifted, parts, total, frames)


def third_kernel(frames, members, where, mixer, total, own, *rest):
    pairs, (result, halo, every, grads, norms) = rest[:8], rest[8:]
    sums, given = [total] + [pair.at[0] for pair in pairs[1:]], [pair.at[1] for pair in pairs]
    mean, inv = statistics(sums, mixer[...], members)
    first = second = None
    for slot, side in SIDES:
        for frame in range(frames):
            normed = (sums[2 * slot + side][frame].astype(F32) - mean) * inv
            gate = gate_of(normed)
            grad = given[2 * slot + side][frame].astype(F32) * gate * (1.0 + normed * (1.0 - gate))
            first = grad if first is None else first + grad
            second = grad * normed if second is None else second + grad * normed
            norms[slot, side, frame] = normed
            grads[slot, side, frame] = grad
            if slot == 0 and side == 0:
                result[frame] = (own[frame].astype(F32) + normed * gate).astype(BF16)
    first = group_total(mixer[...], jnp.sum(first, axis=1, keepdims=True))[:, :1] / members
    second = group_total(mixer[...], jnp.sum(second, axis=1, keepdims=True))[:, :1] / members
    for slot, side in SIDES:
        for frame in range(frames):
            cells = grads[slot, side, frame] - first - norms[slot, side, frame] * second
            every[slot, side, frame] = (cells * inv).astype(BF16)
    ready = lambda slot, side, frame: every[slot, side, frame]
    for place in range(frames + 2):
        halo[place] = neighbour_block(ready, place, 0, frames, where)


def fourth_kernel(frames, where, weight, norm, *rest):
    halos, (grad, shifted) = rest[:8], rest[8:]
    channels = norm.shape[1]
    for part in range(4):
        owner = jnp.bitwise_xor(where[2], part)
        block = lambda place, side: halos[2 * part + side][place]
        fill_shifted(shifted, block, channels, frames, True, owner * channels, 4 * channels)
    out = back_product(weight, shifted, frames)
    for frame in range(frames):
        normed = norm[frame]
        gate = gate_of(normed)
        cells = out[:, frame * LANES : (frame + 1) * LANES]
        grad[frame] = (cells * gate * (1.0 + normed * (1.0 - gate))).astype(BF16)


def back_product(weight, shifted, frames):
    depth = weight.shape[2]
    out = None
    for tap_frame in range(3):
        for side in range(2):
            window = shifted[
                pl.ds(side * depth, depth), pl.ds((2 - tap_frame) * LANES, frames * LANES)
            ]
            term = jnp.dot(weight[tap_frame * 2 + side], window, preferred_element_type=F32)
            out = term if out is None else out + term
    return out


def fifth_kernel(frames, members, where, mixer, scale, *rest):
    sums, grads, (out, every) = rest[:8], rest[8:16], rest[16:]
    mean, inv = scale[:, :1], scale[:, 1:2]
    norm = lambda slot, side, frame: (sums[2 * slot + side][frame] - mean) * inv
    first = second = None
    for slot, side in SIDES:
        for frame in range(frames):
            cells = grads[2 * slot + side][frame].astype(F32)
            first = cells if first is None else first + cells
            term = cells * norm(slot, side, frame)
            second = term if second is None else second + term
    first = group_total(mixer[...], jnp.sum(first, axis=1, keepdims=True))[:, :1] / members
    second = group_total(mixer[...], jnp.sum(second, axis=1, keepdims=True))[:, :1] / members
    for slot, side in SIDES:
        for frame in range(frames):
            cells = grads[2 * slot + side][frame].astype(F32)
            cells = cells - first - norm(slot, side, frame) * second
            cells = (cells * inv).astype(BF16)
            every[slot, side, frame] = cells
            if slot in (0, 3) and side == 0:
                out[slot // 3, frame] = cells


def pad_kernel(frames, where, *rest):
    pieces, padded = rest[:8], rest[8]
    fill_padded(padded, pick(pieces), frames, where, pieces[0].shape[1])


def lanes_of(where, slot, frames, frame):
    start = jnp.bitwise_xor(where[0], slot) * frames + frame
    return pl.ds(pl.multiple_of(start * LANES, LANES), LANES)


def fill_padded(padded, inputs, frames, where, channels):
    zeros = jnp.zeros((padded.shape[0], LANES), padded.dtype)
    padded[:, pl.ds(0, LANES)] = zeros
    padded[:, pl.ds(padded.shape[1] - LANES, LANES)] = zeros
    for slot, side in SIDES:
        for frame in range(frames):
            cells = inputs(slot, side, frame)
            for tap_col in range(3):
                rows = pl.ds((side * 3 + tap_col) * channels, channels)
                padded[rows, lanes_of(where, slot, frames, frame + 1)] = shift(cells, tap_col)


def weight_step(grads, frames, where, channels, out, padded, full, ready, sent, finish=None):
    under_rows = -(-4 * channels // LANES) * LANES
    gap = under_rows - 4 * channels
    full[pl.ds(4 * channels, gap), :] = jnp.zeros((gap, full.shape[1]), full.dtype)
    for slot, side in SIDES:
        for frame in range(frames):
            for part in range(4):
                owner = jnp.bitwise_xor(where[2], part)
                rows = pl.ds(pl.multiple_of(side * under_rows + owner * channels, 16), channels)
                full[rows, lanes_of(where, slot, frames, frame)] = grads(slot, side, part, frame)
    copies = []
    for tap_frame in range(3):
        window = padded[:, pl.ds(tap_frame * LANES, full.shape[1])]
        both = lax.dot_general(window, full[...], (((1,), (1,)), ((), ())), preferred_element_type=F32)
        mine, theirs = both[:, : 4 * channels], both[:, under_rows:]
        for tap_col in range(3):
            upper = slice(tap_col * channels, (tap_col + 1) * channels)
            under = slice((3 + tap_col) * channels, (4 + tap_col) * channels)
            ready[tap_frame, 3 + tap_col] = mine[upper] + theirs[under]
            ready[tap_frame, 3 * other_tap(where, False) + tap_col] = mine[under]
            ready[tap_frame, 3 * other_tap(where, True) + tap_col] = theirs[upper]
        copies.append(
            pltpu.make_async_copy(ready.at[tap_frame], out.at[pl.ds(9 * tap_frame, 9)], sent.at[tap_frame])
        )
        copies[-1].start()
    if finish is not None:
        finish()
    for copy in copies:
        copy.wait()


def pad_hidden_kernel(frames, where, hidden, padded):
    inputs = lambda slot, side, frame: hidden[slot, side, frame]
    fill_padded(padded, inputs, frames, where, hidden.shape[3])


def weight_kernel(frames, where, padded, every, *rest):
    own, far, (out, full, ready, sent) = rest[:6], rest[6:12], rest[12:]
    channels = every.shape[3]

    def grads(slot, side, part, frame):
        if part == 0:
            return every[slot, side, frame]
        if slot == 0:
            return own[2 * (part - 1) + side][frame + 1]
        return far[2 * (slot - 1) + side][part - 1, frame]

    weight_step(grads, frames, where, channels, out, padded, full, ready, sent)


def last_kernel(frames, where, weight, cotangent, padded, every, *rest):
    far, (out, back, full, shifted, ready, sent) = rest[:8], rest[8:]
    channels = weight.shape[1]

    def grads(slot, side, part, frame):
        if part == 0:
            return every[slot, side, frame]
        return far[2 * slot + side][part - 1, frame]

    def finish():
        for part in range(4):
            pieces = lambda slot, side, frame: grads(slot, side, part, frame)
            block = lambda place, side: neighbour_block(pieces, place, side, frames, where)
            owner = jnp.bitwise_xor(where[2], part)
            fill_shifted(shifted, block, channels, frames, True, owner * channels, 4 * channels)
        grown = back_product(weight, shifted, frames)
        for frame in range(frames):
            cells = cotangent[frame].astype(F32) + grown[:, frame * LANES : (frame + 1) * LANES]
            back[frame] = cells.astype(BF16)

    weight_step(grads, frames, where, channels, out, padded, full, ready, sent, finish)


def swap(values):
    return lax.ppermute(values, "row", [(0, 1), (1, 0)])


def hop(values, axis, step):
    return lax.ppermute(values, axis, [(i, i ^ step) for i in range(4)])


def over_channels(parts):
    return parts[0] + sum(hop(parts[k], "chan", k).astype(F32) for k in range(1, 4))


def hops(values):
    return [hop(values, "frame", k) for k in range(1, 4)]


def with_sides(pieces):
    return [values for piece in pieces for values in (piece, swap(piece))]


def around(values):
    return with_sides([values] + hops(values))


def shards_paired(activations, conv_first, conv_second, cotangent):
    channels, frames = activations.shape[:2]
    cells = frames * LANES
    count = lax.axis_size("frame")
    wide = 4 * channels
    members = (C // GROUPS) * cells * count * 2
    my_frame, my_row, place = (lax.axis_index(a) for a in ("frame", "row", "chan"))
    where = jnp.stack([my_frame, my_row, place]).astype(jnp.int32)
    group = np.arange(channels) // (C // GROUPS)
    mixer = jnp.asarray((group[:, None] == group[None, :]).astype(np.float32))
    conv_cost = dict(flops=2 * channels * wide * 18 * cells, reads=18 * channels * wide * 2)

    block = (frames, channels, LANES)
    sums_shape = jax.ShapeDtypeStruct(block, F32)
    cells_shape = jax.ShapeDtypeStruct(block, BF16)
    parts_shape = [sums_shape] + [jax.ShapeDtypeStruct(block, LINK)] * 3
    span = (frames + 2) * LANES
    shifted = pltpu.VMEM((6 * channels, span), BF16)
    wide_shifted = pltpu.VMEM((6 * wide, span), BF16)
    total = pltpu.VMEM((wide, cells), F32)

    by_frame = lambda values: values.transpose(1, 2, 0, 3).reshape(block)
    restore = lambda values: values.reshape(frames, 1, channels, LANES).transpose(2, 0, 1, 3)
    inputs, given = by_frame(activations), by_frame(cotangent)
    behind_shape = jax.ShapeDtypeStruct((6, channels, 3 * wide), BF16)
    prepared = call(
        prepare_kernel, [behind_shape, behind_shape], (where, conv_first, conv_second), reads=6000000
    )
    near, (behind_first, behind_second) = lax.optimization_barrier((hops(inputs), prepared))
    every_input = with_sides([inputs] + near)
    parts = call(
        functools.partial(first_kernel, frames), parts_shape,
        (where, conv_first, *every_input), (shifted, total), **conv_cost,
    )
    sums = over_channels(parts)
    first_sums = around(sums)
    hidden, norm, scale, *parts = call(
        functools.partial(second_kernel, frames, members),
        [
            jax.ShapeDtypeStruct((count, 2, *block), BF16),
            sums_shape,
            jax.ShapeDtypeStruct((channels, LANES), F32),
            *parts_shape,
        ],
        (where, conv_second, mixer, *first_sums), (shifted, total), **conv_cost,
    )
    padded_shape = jax.ShapeDtypeStruct((6 * channels, (frames * count + 2) * LANES), BF16)
    (padded_inputs,) = call(
        functools.partial(pad_kernel, frames), [padded_shape], (where, *every_input), reads=2000000
    )
    far = [hop(parts[k], "chan", k) for k in range(1, 4)]
    far, padded_inputs = lax.optimization_barrier((far, padded_inputs))
    sums = parts[0] + sum(values.astype(F32) for values in far)
    every_pair = around(jnp.stack([sums.astype(BF16), given]))
    every_shape = jax.ShapeDtypeStruct((count, 2, *block), BF16)
    result, halo, every_second = call(
        functools.partial(third_kernel, frames, members),
        [cells_shape, jax.ShapeDtypeStruct((frames + 2, channels, LANES), BF16), every_shape],
        (where, mixer, sums, inputs, *every_pair),
        (pltpu.VMEM((4, 2, *block), F32), pltpu.VMEM((4, 2, *block), F32)), grant=24,
    )
    (padded_hidden,) = call(
        functools.partial(pad_hidden_kernel, frames), [padded_shape], (where, hidden), reads=2000000
    )
    far = [hop(halo, "chan", k) for k in range(1, 4)]
    far, padded_hidden = lax.optimization_barrier((far, padded_hidden))
    halos = [halo] + far
    sides = with_sides(halos)
    (grad,) = call(
        functools.partial(fourth_kernel, frames), [cells_shape],
        (where, behind_second, norm, *sides), (wide_shifted,), **conv_cost,
    )
    grad_first, every_first = call(
        functools.partial(fifth_kernel, frames, members),
        [jax.ShapeDtypeStruct((2, *block), BF16), every_shape],
        (where, mixer, scale, *first_sums, *around(grad)),
    )
    rest = jnp.stack([values[1:-1] for values in halos[1:]])
    rest, grad_first = lax.optimization_barrier((rest, grad_first))
    far = [hop(grad_first, "chan", k) for k in range(1, 4)]
    far = [jnp.stack([values[k] for values in far]) for k in range(2)]
    near, _ = lax.optimization_barrier((hops(rest), far))
    full = pltpu.VMEM((-(-wide // LANES) * LANES + wide, cells * count), BF16)
    grad_shape = jax.ShapeDtypeStruct((27, channels, wide), F32)
    grad_spec = pl.BlockSpec(memory_space=pl.ANY)
    staging = (pltpu.VMEM((3, 9, channels, wide), F32), pltpu.SemaphoreType.DMA((3,)))
    grad_cost = dict(flops=2 * 18 * channels * wide * cells * count * 2, reads=8000000)
    (second_grad,) = call(
        functools.partial(weight_kernel, frames), [grad_shape],
        (where, padded_hidden, every_second, *sides[2:], *with_sides(near)), (full, *staging),
        specs=[grad_spec], grant=32, **grad_cost,
    )
    near, second_grad = lax.optimization_barrier(([hop(far[0], "frame", k) for k in (1, 2)], second_grad))
    first_grad, input_grad = call(
        functools.partial(last_kernel, frames), [grad_shape, cells_shape],
        (where, behind_first, given, padded_inputs, every_first, *with_sides([far[0], *near, far[1]])),
        (full, wide_shifted, *staging),
        specs=[grad_spec, pl.BlockSpec(memory_space=pltpu.VMEM)], grant=32, **grad_cost,
    )
    return (restore(result), restore(input_grad), first_grad, second_grad)


def paired(mesh):
    return mesh.shape["frame"] == 4 and mesh.shape["row"] == 2 and mesh.shape["chan"] == 4


def solution(mesh):
    return jax.shard_map(
        shards_paired if paired(mesh) else shards_general,
        mesh=mesh,
        in_specs=(
            P("chan", "frame", "row", None),
            P(None, "chan", None),
            P(None, "chan", None),
            P("chan", "frame", "row", None),
        ),
        out_specs=(
            P("chan", "frame", "row", None),
            P("chan", "frame", "row", None),
            P(None, "chan", None),
            P(None, "chan", None),
        ),
        check_vma=False,
    )
```
